32 devices in a mesh: sample: 2 (over y), grid: 16 (over z, x, core).
Axes of the slice: x: 2, y: 2, z: 4, core: 2. Of those that a mesh axis runs over, the one named last changes fastest.
Arguments:
- orbitals: float32 [64, 16, 32, 128], P('sample', 'grid'), parts along dimension 0, may hold values from -6 to 6
- cotangent: float32 [64, 16, 32, 128], P('sample', 'grid'), parts along dimension 0, may hold values from -6 to 6
- potential: float32 [16, 32, 128], P('grid'), may hold values from 0 to 1.5
- cheb_coef: float32 [4], replicated, may hold values from 0.3 to 1
- energy: float32 [32], replicated, may hold values from 0.5 to 2
- proj_cell: int32 [32768], P('grid'), may hold values from 0 to 4095, as said below
- proj_atom: int32 [32768], P('grid'), may hold values from 0 to 31, as said below
- proj_value: float32 [32768], P('grid'), may hold values from -0.1875 to 0.1875
Outputs:
- grad_orbitals: float32 [64, 16, 32, 128], P('sample', 'grid'), parts along dimension 0
- grad_potential: float32 [32, 32, 128], P(('sample', 'grid')), parts along dimension 0
- grad_energy: float32 [64], P(('sample', 'grid')), parts along dimension 0
The draws below stay inside these ranges and needn't reach their ends.
There are 2 independent parts, one for each index of `sample`. The reference program is written for one: setup_inputs(seed, part) draws one part's arguments, and reference() takes and returns one part's arrays. A program takes and returns all parts, laid end to end along the dimension named above; an argument that names none is the same for every part. Nothing has to cross between parts.
Inputs may be any that keep to these rules, and one draw needn't show every extreme that they name: Point i lies in the grid slab of device i // 2048 of the grid axis; proj_cell[i] = x * 32 * 128 + y * 128 + z with x counted within that slab; points may repeat. `proj_atom`: atom a is homed on grid device a // 2; the atom of point i is homed on device i // 2048 or on one of its two neighbours, the devices taken as a closed loop.
All inputs are finite; a program needn't handle non-finite values.
Results may differ from the reference program's by a relative error of at most 0.00029.
Values sent between devices are 32-bit elements; how exact they have to be, the bound alone decides.
No kernel may reach another device: no remote copies, remote signals or barrier semaphores. Data moves between devices by JAX's collectives and lax.ppermute only.
A program may use at most 64 MiB of HBM per device.

```python
import jax
import jax.numpy as jnp

ORB = 32
NY = 32
NZ = 128
CX = 1
PTS_ATOM = 1024
TERMS = 4
ATOM_DEV = 2
PTS_DEV = 2048
ATOMS = 32
NX = 16
N_GRID = 16


def draw_proj_cell(key, part):
    key = jax.random.fold_in(key, 11)
    total = PTS_DEV * (ATOMS // ATOM_DEV)
    cell_count = CX * NY * NZ
    position = jnp.arange(total, dtype=jnp.int32)
    within = position % PTS_DEV
    random_cell = jax.random.randint(key, (total,), 0, cell_count, dtype=jnp.int32)
    return jnp.where(within == 0, 0, jnp.where(within == PTS_DEV - 1, cell_count - 1, random_cell))


def draw_proj_atom(key, part):
    key = jax.random.fold_in(key, 23)
    total = PTS_DEV * (ATOMS // ATOM_DEV)
    devices = ATOMS // ATOM_DEV
    position = jnp.arange(total, dtype=jnp.int32)
    device_of = position // PTS_DEV
    within = position % PTS_DEV
    key_shift, key_rank = jax.random.split(key)
    offset = jax.random.randint(key_shift, (total,), -1, 2, dtype=jnp.int32)
    rank_in = jax.random.randint(key_rank, (total,), 0, ATOM_DEV, dtype=jnp.int32)
    offset = jnp.where(within == 0, -1, jnp.where(within == 1, 1, offset))
    rank_in = jnp.where(within == 0, 0, jnp.where(within == 1, ATOM_DEV - 1, rank_in))
    return (device_of + offset + devices) % devices * ATOM_DEV + rank_in


def shard_levels(own_key, dims, cuts, low, largest):
    gain = 1.0
    for dim, parts in cuts:
        draws = jax.random.uniform(jax.random.fold_in(jax.random.fold_in(own_key, 6), dim), (parts,), jnp.float32, low / len(cuts), largest / len(cuts))
        gain = gain * jnp.repeat(jnp.exp(draws), dims[dim] // parts).reshape((-1,) + (1,) * (len(dims) - 1 - dim))
    return gain


def centred(key, dims, deviation, limit, shards=(), kind=jnp.bfloat16):
    array = jax.random.normal(key, dims, jnp.float32) * deviation
    if len(shards) > 0:
        array = shard_levels(key, dims, shards, -0.22, 0.18) * array
    return jnp.clip(array, min=-limit, max=limit).astype(kind)


def setup_inputs(seed: int = 0, part: int = 0) -> dict:
    arg_keys = jax.random.split(jax.random.key(seed), 9)
    part_keys = jax.random.split(jax.random.fold_in(arg_keys[8], part), 9)
    orbitals = centred(part_keys[0], (ORB, NX, NY, NZ), 1.0, 6.0, ((1, 16),), jnp.float32)
    cotangent = centred(part_keys[1], (ORB, NX, NY, NZ), 1.0, 6.0, ((1, 16),), jnp.float32)
    potential = jnp.clip(1.5 * jax.random.uniform(arg_keys[2], (NX, NY, NZ), jnp.float32) ** shard_levels(arg_keys[2], (NX, NY, NZ), ((0, 16),), -0.2, 0.2), 0.0, 1.5)
    cheb_coef = jnp.clip(jax.random.uniform(arg_keys[3], (TERMS,), jnp.float32, 0.3, 1.0), 0.3, 1.0)
    energy = jnp.clip(jax.random.uniform(arg_keys[4], (ATOMS,), jnp.float32, 0.5, 2.0), 0.5, 2.0)
    proj_cell = draw_proj_cell(jax.random.fold_in(arg_keys[8], 71), part)
    proj_atom = draw_proj_atom(jax.random.fold_in(arg_keys[8], 71), part)
    proj_value = centred(arg_keys[7], (PTS_DEV * N_GRID,), PTS_ATOM ** -0.5, 0.1875, ((0, 16),), jnp.float32)
    return {"orbitals": orbitals, "cotangent": cotangent, "potential": potential, "cheb_coef": cheb_coef, "energy": energy, "proj_cell": proj_cell, "proj_atom": proj_atom, "proj_value": proj_value}


spectral_center = 4.5
spectral_half = 4.5


def apply_operator(field, potential, energy, global_cell, proj_atom, proj_value):
    rows_count = field.shape[0]
    beside = jnp.roll(field, 1, axis=1) + jnp.roll(field, -1, axis=1)
    beside = beside + jnp.roll(field, 1, axis=2) + jnp.roll(field, -1, axis=2)
    beside = beside + jnp.roll(field, 1, axis=3) + jnp.roll(field, -1, axis=3)
    kinetic = -0.5 * (beside - 6.0 * field)
    flat = field.reshape(rows_count, -1)
    picked = flat[:, global_cell] * proj_value[None, :]
    coef = jax.ops.segment_sum(picked.T, proj_atom, num_segments=energy.shape[0]).T
    spread = (coef * energy[None, :])[:, proj_atom] * proj_value[None, :]
    nonlocal_part = jnp.zeros_like(flat).at[:, global_cell].add(spread).reshape(field.shape)
    result = (kinetic + potential[None] * field + nonlocal_part - spectral_center * field) / spectral_half
    return result, coef


def reference(orbitals, cotangent, potential, cheb_coef, energy, proj_cell, proj_atom, proj_value):
    position = jnp.arange(proj_cell.shape[0], dtype=jnp.int32)
    global_cell = ((position // PTS_DEV) * (CX * NY * NZ) + proj_cell).astype(jnp.int32)

    def oper(field):
        return apply_operator(field, potential, energy, global_cell, proj_atom, proj_value)

    term_zero = orbitals
    term_one, proj_zero = oper(term_zero)
    image, proj_one = oper(term_one)
    term_two = 2.0 * image - term_zero
    back_three = cheb_coef[3] * cotangent
    image, coef_three = oper(back_three)
    back_two = cheb_coef[2] * cotangent + 2.0 * image
    image, coef_two = oper(back_two)
    back_one = cheb_coef[1] * cotangent + 2.0 * image - back_three
    image, coef_one = oper(back_one)
    flat_two = term_two.reshape(term_two.shape[0], -1)
    proj_two = jax.ops.segment_sum((flat_two[:, global_cell] * proj_value[None, :]).T, proj_atom, num_segments=energy.shape[0]).T
    grad_orbitals = cheb_coef[0] * cotangent + image - back_two
    grad_potential = jnp.sum(back_one * term_zero + 2.0 * back_two * term_one + 2.0 * back_three * term_two, axis=0) / spectral_half
    grad_energy = jnp.sum(coef_one * proj_zero + 2.0 * coef_two * proj_one + 2.0 * coef_three * proj_two, axis=0) / spectral_half
    return grad_orbitals, grad_potential, grad_energy
```

```python
import functools

import jax
import jax.numpy as jnp
from jax import lax
from jax.experimental import pallas as pl
from jax.experimental.pallas import tpu as pltpu
from jax.sharding import PartitionSpec as P

spectral_center = 4.5
spectral_half = 4.5

GROUP = 4
LANES = 128
F32 = jnp.float32


def call(body, outs, *args, scratch=(), smem=(), any_args=(), any_outs=()):
    in_specs, operands = [], []
    for n, a in enumerate(args):
        if n in smem:
            in_specs.append(pl.BlockSpec(memory_space=pltpu.SMEM))
        elif n in any_args:
            in_specs.append(pl.BlockSpec(memory_space=pl.ANY))
        else:
            in_specs.append(pl.BlockSpec(memory_space=pltpu.VMEM))
            a = pltpu.with_memory_space_constraint(a, pltpu.VMEM)
        operands.append(a)
    out_shape, out_specs = [], []
    for n, shape in enumerate(outs):
        if n in any_outs:
            out_shape.append(jax.ShapeDtypeStruct(shape, F32))
            out_specs.append(pl.BlockSpec(memory_space=pl.ANY))
        else:
            out_shape.append(pltpu.VMEM(shape, F32))
            out_specs.append(pl.BlockSpec(memory_space=pltpu.VMEM))
    return pl.pallas_call(
        body,
        out_shape=out_shape,
        in_specs=in_specs,
        out_specs=out_specs,
        scratch_shapes=list(scratch),
        compiler_params=pltpu.CompilerParams(vmem_limit_bytes=16 << 20),
    )(*operands)


def lane_iota(shape):
    return lax.broadcasted_iota(jnp.int32, shape, len(shape) - 1)


def prep_kernel(devices, atoms, idx, cell, atom, value, pot, out):
    rows = cell.shape[0]
    atom_dev = atoms // devices
    shifted = atom[...] + (atoms - (idx[0] - 1) * atom_dev)
    shifted = jnp.where(shifted >= 2 * atoms, shifted - 2 * atoms, shifted)
    slot = jnp.where(shifted >= atoms, shifted - atoms, shifted)
    out[0:rows, :] = cell[...].astype(F32)
    out[rows : 2 * rows, :] = slot.astype(F32)
    out[2 * rows : 3 * rows, :] = value[...]
    out[3 * rows :, :] = pot[...]


def pack_kernel(rows, idx, field, *refs):
    outs, sems = refs[:GROUP], refs[GROUP]
    k = lax.rem(idx[0], GROUP)
    copies = []
    for j in range(GROUP):
        first = pl.multiple_of((k ^ j) * rows, rows)
        copies.append(
            pltpu.make_async_copy(field.at[pl.ds(first, rows)], outs[j], sems.at[j])
        )
    for copy in copies:
        copy.start()
    for copy in copies:
        copy.wait()


def dense_kernel(ny, slots, idx, *refs):
    ins, out = refs[:GROUP], refs[GROUP]
    k = lax.rem(idx[0], GROUP)
    rows = (ins[0].shape[0] - ny) // 3
    count = rows * LANES
    place = lax.broadcasted_iota(jnp.int32, (ny * 8, count), 0)
    column = lax.broadcasted_iota(jnp.int32, (LANES, count), 0)
    for j in range(GROUP):
        src = ins[j]
        flat = lambda part: jnp.concatenate(
            [src[part * rows + r : part * rows + r + 1, :] for r in range(rows)], axis=1
        )
        cell = flat(0).astype(jnp.int32)
        slot = flat(1).astype(jnp.int32)
        value = flat(2)
        code = (cell // LANES) * 8 + slot
        z = cell % LANES
        left = jnp.where(place == code, 1.0, 0.0).astype(jnp.bfloat16)
        hit = column == z
        high = value.astype(jnp.bfloat16).astype(F32)
        rest = value - high
        middle = rest.astype(jnp.bfloat16).astype(F32)
        low = rest - middle
        dense = None
        for piece in (low, middle, high):
            right = jnp.where(hit, piece, 0.0).astype(jnp.bfloat16)
            term = lax.dot_general(
                left, right, (((1,), (1,)), ((), ())), preferred_element_type=F32
            )
            dense = term if dense is None else dense + term
        first = pl.multiple_of((k ^ j) * ny, ny)
        out[pl.ds(first, ny)] = dense.reshape(ny, 8, LANES)
        pot = (src[3 * rows :, :] - (spectral_center - 3.0)) * (1.0 / spectral_half)
        out[pl.ds(first, ny), slots : slots + 1, :] = pot.reshape(ny, 1, LANES)


def edge_tiles(tile, width, shift):
    lane = lane_iota(tile.shape)
    above = jnp.where(lane < width, pltpu.roll(tile, LANES - shift, 1), 0.0)
    below = jnp.where((lane >= shift) & (lane < shift + width), pltpu.roll(tile, shift, 1), 0.0)
    return above, below


def coef_tile(sums, slots, atom_dev):
    atoms = (GROUP + 2) * atom_dev
    lane = lane_iota((8, LANES))
    tile = jnp.zeros((8, LANES), F32)
    for t in range(atoms):
        total = None
        for p in range(GROUP):
            slot = t - p * atom_dev
            if 0 <= slot < slots:
                total = sums[p][slot] if total is None else total + sums[p][slot]
        tile = jnp.where(lane == t, jnp.sum(total, axis=1, keepdims=True), tile)
    return tile


def relay_kernel(ny, atom_dev, idx, *refs):
    slots = 3 * atom_dev
    ins, (dense, field, tile_out, up, down, sums) = refs[:GROUP], refs[GROUP:]
    k = lax.rem(idx[0], GROUP)
    un = 8
    for j in range(GROUP):
        p = k ^ j
        src = ins[j]

        def body(yb, accs, src=src, p=p):
            accs = list(accs)
            for yy in range(un):
                y = yb * un + yy
                v = src[pl.ds(y, 8, stride=ny), :]
                row = p * ny + y
                field[row] = v
                for s in range(slots):
                    accs[s] = accs[s] + v * dense[row, s : s + 1, :]
            return tuple(accs)

        zero = jnp.zeros((8, LANES), F32)
        accs = lax.fori_loop(0, ny // un, body, (zero,) * slots)
        for s in range(slots):
            sums[p * slots + s] = accs[s]
    parts = [[sums[p * slots + s] for s in range(slots)] for p in range(GROUP)]
    tile = coef_tile(parts, slots, atom_dev)
    tile_out[...] = tile
    above, below = edge_tiles(tile, 2 * atom_dev, GROUP * atom_dev)
    up[ny] = above
    down[ny] = below
    up[0:ny] = field[(GROUP - 1) * ny : GROUP * ny]
    down[0:ny] = field[0:ny]


def step_kernel(kind, ny, devices, atoms, *refs):
    atom_dev = atoms // devices
    slots = 3 * atom_dev
    refs = list(refs)
    take = lambda count: [refs.pop(0) for _ in range(count)]
    idx, cheb, energy, dense, field, tile_in, below, above = take(8)
    if kind == "b1":
        (other,) = take(1)
    elif kind == "t2":
        other, full_zero, b1, tile_b1, b2, tile_b2, cot, full_cot = take(8)
    elif kind == "out":
        other, cot = take(2)
    if kind in ("b2", "t1"):
        new, tile_out, up, down, full_out = refs
    elif kind == "b1":
        new, tile_out, up, down = refs
    elif kind == "t2":
        gp, e_out, e_up, e_down = refs
    else:
        (new,) = refs

    full = tile_in[...] + below[ny] + above[ny]
    if kind in ("b2", "t1"):
        full_out[...] = full
    c0, c1, c2, c3 = [cheb[n] for n in range(4)]
    one = jnp.float32(1.0)
    keep, scale, mix = {
        "t1": (None, one, None),
        "t2": (None, 2.0 * one, -one),
        "b2": (c2, 2.0 * c3, None),
        "b1": (None, 2.0 * one, c1 - c3),
        "out": (None, one, -one),
    }[kind]
    first_atom = lax.rem((idx[0] // GROUP) * GROUP + devices - 1, devices) * atom_dev
    spread = []
    for t in range((GROUP + 2) * atom_dev):
        e = energy[lax.rem(first_atom + t, atoms)] * (scale * (1.0 / spectral_half))
        spread.append(jnp.broadcast_to(full[:, t : t + 1], (8, LANES)) * e)
    side = scale * (-0.5 / spectral_half)
    un = 8
    sums = []
    for p in range(GROUP):

        def body(yb, accs, p=p):
            accs = list(accs)
            rows = []
            for yy in range(un):
                y = yb * un + yy
                row = p * ny + y
                v = field[row]
                later = field[p * ny + lax.rem(y + 1, ny)]
                earlier = field[p * ny + lax.rem(y + ny - 1, ny)]
                under = field[row - ny] if p > 0 else below[y]
                over = field[row + ny] if p < GROUP - 1 else above[y]
                beside = (later + earlier) + (under + over)
                beside = beside + (pltpu.roll(v, 1, 1) + pltpu.roll(v, LANES - 1, 1))
                pot = dense[row, slots : slots + 1, :] * scale
                if keep is not None:
                    pot = pot + keep
                weights = [dense[row, s : s + 1, :] for s in range(slots)]
                a = spread[p * atom_dev] * weights[0]
                for s in range(1, slots):
                    a = a + spread[p * atom_dev + s] * weights[s]
                x = v * pot + beside * side + a
                if mix is not None:
                    x = x + other[row] * mix
                if kind == "out":
                    x = x + cot[row] * c0
                    new[pl.ds(p * 8 * ny + y, 8, stride=ny), :] = x
                elif kind == "t2":
                    g = b1[row] * other[row] + 2.0 * (b2[row] * v)
                    g = g + (2.0 * c3) * (cot[row] * x)
                    rows.append(jnp.sum(g, axis=0, keepdims=True))
                else:
                    new[row] = x
                if kind != "out":
                    for s in range(slots):
                        accs[s] = accs[s] + x * weights[s]
            if kind == "t2":
                start = pl.multiple_of(p * ny + yb * un, un)
                gp[pl.ds(start, un), :] = jnp.concatenate(rows, axis=0) * (1.0 / spectral_half)
            return tuple(accs)

        zero = jnp.zeros((8, LANES), F32)
        init = () if kind == "out" else (zero,) * slots
        sums.append(lax.fori_loop(0, ny // un, body, init))
    if kind == "out":
        return
    tile = coef_tile(sums, slots, atom_dev)
    if kind == "t2":
        e = tile_b1[...] * full_zero[...] + 2.0 * (tile_b2[...] * full)
        e = e + (2.0 * c3) * (full_cot[...] * tile)
        e = jnp.sum(e, axis=0, keepdims=True) * (1.0 / spectral_half)
        e = jnp.broadcast_to(e, (8, LANES))
        e_out[...] = e
        lane = lane_iota(e.shape)
        shift = GROUP * atom_dev
        own = (lane >= atom_dev) & (lane < shift + atom_dev)
        e_up[...] = jnp.where(own, pltpu.roll(e, LANES - shift, 1), 0.0)
        e_down[...] = jnp.where(own, pltpu.roll(e, shift, 1), 0.0)
        return
    tile_out[...] = tile
    over, under = edge_tiles(tile, 2 * atom_dev, GROUP * atom_dev)
    up[ny] = over
    down[ny] = under
    up[0:ny] = new[(GROUP - 1) * ny : GROUP * ny]
    down[0:ny] = new[0:ny]


def sums_kernel(ny, idx, gp, e, e_below, e_above, *outs):
    k = lax.rem(idx[0], GROUP)
    total = e[...] + e_below[...] + e_above[...]
    for j in range(GROUP):
        first = pl.multiple_of((k ^ j) * ny, ny)
        outs[j][0:ny, :] = gp[pl.ds(first, ny), :]
        outs[j][ny:, :] = total


def final_kernel(ny, atom_dev, idx, *refs):
    blocks, parts = refs[:GROUP], refs[GROUP : 2 * GROUP]
    out, gp, e_out, sems = refs[2 * GROUP :]
    k = lax.rem(idx[0], GROUP)
    rows = 8 * ny
    copies = []
    for j in range(GROUP):
        own = pl.ds(pl.multiple_of(k * rows, rows), rows)
        src = blocks[0].at[own] if j == 0 else blocks[j]
        first = pl.multiple_of((k ^ j) * rows, rows)
        copies.append(pltpu.make_async_copy(src, out.at[pl.ds(first, rows)], sems.at[j]))
    for copy in copies:
        copy.start()
    total = (parts[0][...] + parts[1][...]) + (parts[2][...] + parts[3][...])
    gp[...] = total[0:ny]
    e = total[ny:]
    picked = e
    for n in range(GROUP):
        picked = jnp.where(k == n, pltpu.roll(e, LANES - (n + 1) * atom_dev, 1), picked)
    e_out[...] = picked
    for copy in copies:
        copy.wait()


def per_device(orbitals, cotangent, potential, cheb_coef, energy, proj_cell, proj_atom, proj_value):
    orb, _, ny, nz = orbitals.shape
    devices = lax.axis_size("grid")
    slabs = devices // GROUP
    atoms = energy.shape[0]
    atom_dev = atoms // devices
    points = proj_cell.shape[0] // LANES
    assert orb == 8 * GROUP and nz == LANES and devices % GROUP == 0
    idx = lax.axis_index("grid").astype(jnp.int32).reshape(1)
    block = 8 * ny
    plane = GROUP * ny

    def near(x, j):
        return lax.ppermute(x, "grid", [(a, a ^ j) for a in range(devices)])

    to_above = [
        (GROUP * s + m, GROUP * ((s + 1) % slabs) + m) for s in range(slabs) for m in range(GROUP)
    ]
    to_below = [(b, a) for a, b in to_above]

    def halo(up, down):
        return lax.ppermute(up, "grid", to_above), lax.ppermute(down, "grid", to_below)

    def gather(blocks):
        return [blocks[0]] + [near(blocks[j], j) for j in range(1, GROUP)]

    (points_own,) = call(
        functools.partial(prep_kernel, devices, atoms),
        [(3 * points + ny, LANES)],
        idx,
        proj_cell.reshape(points, LANES),
        proj_atom.reshape(points, LANES),
        proj_value.reshape(points, LANES),
        potential.reshape(ny, LANES),
        smem=(0,),
    )
    points_all = [points_own] + [near(points_own, j) for j in range(1, GROUP)]

    def pack(field):
        return call(
            functools.partial(pack_kernel, block),
            [(block, LANES)] * GROUP,
            idx,
            field.reshape(orb * ny, LANES),
            scratch=[pltpu.SemaphoreType.DMA((GROUP,))],
            smem=(0,),
            any_args=(1,),
        )

    cot_blocks = gather(pack(cotangent))
    orb_blocks = gather(pack(orbitals))
    (dense,) = call(
        functools.partial(dense_kernel, ny, 3 * atom_dev),
        [(plane, 8, LANES)],
        idx,
        *points_all,
        smem=(0,),
    )
    field_shape, tile_shape, edge_shape = (plane, 8, LANES), (8, LANES), (ny + 1, 8, LANES)

    def relay(blocks):
        return call(
            functools.partial(relay_kernel, ny, atom_dev),
            [field_shape, tile_shape, edge_shape, edge_shape],
            idx,
            *blocks,
            dense,
            scratch=[pltpu.VMEM((GROUP * 3 * atom_dev, 8, LANES), F32)],
            smem=(0,),
        )

    def step(kind, outs, *args):
        return call(
            functools.partial(step_kernel, kind, ny, devices, atoms),
            outs,
            idx,
            cheb_coef,
            energy,
            dense,
            *args,
            smem=(0, 1, 2),
        )

    chain = [field_shape, tile_shape, edge_shape, edge_shape]
    cot, tile_cot, up, down = relay(cot_blocks)
    cot_halo = halo(up, down)
    zero, tile_zero, up, down = relay(orb_blocks)
    zero_halo = halo(up, down)
    b2, tile_b2, up, down, full_cot = step("b2", chain + [tile_shape], cot, tile_cot, *cot_halo)
    b2_halo = halo(up, down)
    t1, tile_t1, up, down, full_zero = step("t1", chain + [tile_shape], zero, tile_zero, *zero_halo)
    t1_halo = halo(up, down)
    b1, tile_b1, up, down = step("b1", chain, b2, tile_b2, *b2_halo, cot)
    b1_halo = halo(up, down)
    gp, e, e_up, e_down = step(
        "t2",
        [(plane, LANES)] + [tile_shape] * 3,
        t1,
        tile_t1,
        *t1_halo,
        zero,
        full_zero,
        b1,
        tile_b1,
        b2,
        tile_b2,
        cot,
        full_cot,
    )
    sums = gather(
        call(
            functools.partial(sums_kernel, ny),
            [(ny + 8, LANES)] * GROUP,
            idx,
            gp,
            e,
            *halo(e_up, e_down),
            smem=(0,),
        )
    )
    (image,) = step("out", [(GROUP * block, LANES)], b1, tile_b1, *b1_halo, b2, cot)
    member = lax.rem(idx[0], GROUP)
    blocks = [image] + [
        near(lax.dynamic_slice_in_dim(image, (member ^ j) * block, block, 0), j)
        for j in range(1, GROUP)
    ]
    out, gp, e = call(
        functools.partial(final_kernel, ny, atom_dev),
        [(orb * ny, LANES), (ny, LANES), tile_shape],
        idx,
        *blocks,
        *sums,
        scratch=[pltpu.SemaphoreType.DMA((GROUP,))],
        smem=(0,),
        any_outs=(0,),
    )
    return out.reshape(orbitals.shape), gp.reshape(potential.shape), e[0, :atom_dev]


def solution(mesh):
    placed = (
        P("sample", "grid", None, None),
        P("sample", "grid", None, None),
        P("grid", None, None),
        P(),
        P(),
        P("grid"),
        P("grid"),
        P("grid"),
    )
    return jax.shard_map(
        per_device,
        mesh=mesh,
        in_specs=placed,
        out_specs=(
            P("sample", "grid", None, None),
            P(("sample", "grid"), None, None),
            P(("sample", "grid")),
        ),
        check_vma=False,
    )
```

```python
import functools

import jax
import jax.numpy as jnp
from jax import lax
from jax.experimental import pallas as pl
from jax.experimental.pallas import tpu as pltpu
from jax.sharding import PartitionSpec as P

spectral_center = 4.5
spectral_half = 4.5

GROUP = 4
LANES = 128
F32 = jnp.float32


def call(body, outs, *args, micros, scratch=(), smem=(), hbm_args=(), hbm_outs=(), smem_outs=()):
    in_specs, operands = [], []
    for n, a in enumerate(args):
        if n in smem:
            in_specs.append(pl.BlockSpec(memory_space=pltpu.SMEM))
        elif n in hbm_args:
            in_specs.append(pl.BlockSpec(memory_space=pltpu.HBM))
            a = pltpu.with_memory_space_constraint(a, pltpu.HBM)
        else:
            in_specs.append(pl.BlockSpec(memory_space=pltpu.VMEM))
            a = pltpu.with_memory_space_constraint(a, pltpu.VMEM)
        operands.append(a)
    out_shape, out_specs = [], []
    for n, shape in enumerate(outs):
        if n in hbm_outs:
            out_shape.append(jax.ShapeDtypeStruct(shape, F32))
            out_specs.append(pl.BlockSpec(memory_space=pltpu.HBM))
        elif n in smem_outs:
            out_shape.append(jax.ShapeDtypeStruct(shape, F32))
            out_specs.append(pl.BlockSpec(memory_space=pltpu.SMEM))
        else:
            out_shape.append(pltpu.VMEM(shape, F32))
            out_specs.append(pl.BlockSpec(memory_space=pltpu.VMEM))
    return pl.pallas_call(
        body,
        out_shape=out_shape,
        in_specs=in_specs,
        out_specs=out_specs,
        scratch_shapes=list(scratch),
        compiler_params=pltpu.CompilerParams(vmem_limit_bytes=16 << 20),
        cost_estimate=pl.CostEstimate(
            flops=int(micros * 1e6), bytes_accessed=int(micros * 3.69e6), transcendentals=0
        ),
    )(*operands)


def lane_iota(shape):
    return lax.broadcasted_iota(jnp.int32, shape, len(shape) - 1)


def prep_kernel(devices, atoms, idx, cheb, energy, cell, atom, value, pot, cot, orb, *refs):
    consts, blocks, (box, sems, box_sems) = refs[0], refs[1:-3], refs[-3:]
    rows = blocks[GROUP].shape[0]
    count, ny = cell.shape[0], pot.shape[0]
    atom_dev = atoms // devices
    k = lax.rem(idx[0], GROUP)
    small = [
        pltpu.make_async_copy(src, box.at[n], box_sems.at[n])
        for n, src in enumerate((cell, atom))
    ]
    copies = []
    for j in range(GROUP):
        first = pl.multiple_of((k ^ j) * rows, rows)
        for n, (src, length) in enumerate(
            (
                (cot.at[pl.ds(first, rows)], (0, rows)),
                (value, (rows, count)),
                (pot, (rows + count, ny)),
            )
        ):
            copies.append(
                pltpu.make_async_copy(src, blocks[j].at[pl.ds(*length)], sems.at[4 * j + n])
            )
    for j in range(GROUP):
        first = pl.multiple_of((k ^ j) * rows, rows)
        copies.append(
            pltpu.make_async_copy(orb.at[pl.ds(first, rows)], blocks[GROUP + j], sems.at[4 * j + 3])
        )
    for copy in small + copies:
        copy.start()
    first_atom = (idx[0] - k - 1) * atom_dev
    for t in range((GROUP + 2) * atom_dev):
        a = first_atom + t
        a = jnp.where(a < 0, a + atoms, jnp.where(a >= atoms, a - atoms, a))
        consts[t : t + 1, :] = jnp.full((1, LANES), energy[a] * (1.0 / spectral_half), F32)
    for n in range(4):
        at = (GROUP + 2) * atom_dev + n
        consts[at : at + 1, :] = jnp.full((1, LANES), cheb[n], F32)
    for copy in small:
        copy.wait()
    shifted = box[1] + (atoms - (idx[0] - 1) * atom_dev)
    shifted = jnp.where(shifted >= 2 * atoms, shifted - 2 * atoms, shifted)
    slot = jnp.where(shifted >= atoms, shifted - atoms, shifted)
    for j in range(GROUP):
        at = rows + count + ny
        blocks[j][at : at + count, :] = box[0].astype(F32)
        blocks[j][at + count : at + 2 * count, :] = slot.astype(F32)
    for copy in copies:
        copy.wait()


def fill_dense(ny, slots, k, ins, out):
    block = 8 * ny
    rows = (ins[0].shape[0] - block - ny) // 3
    rest = block + rows + ny
    half = jnp.bfloat16
    place = lax.broadcasted_iota(jnp.int32, (ny * 8, LANES), 0).astype(F32).astype(half)
    column = lax.broadcasted_iota(jnp.int32, (LANES, LANES), 0).astype(F32).astype(half)
    one, none = jnp.ones((), half), jnp.zeros((), half)
    for j in range(GROUP):
        src = ins[j]
        cell = src[rest : rest + rows, :]
        line = jnp.floor(cell * (1.0 / LANES))
        z = (cell - line * LANES).astype(half)
        code = (line * 8 + src[rest + rows : rest + 2 * rows, :]).astype(half)
        value = src[block : block + rows, :]
        high = value.astype(half)
        low = (value - high.astype(F32)).astype(half)
        left, right = [], []
        for r in range(rows):
            left.append(jnp.where(place == code[r : r + 1, :], one, none))
            hit = column == z[r : r + 1, :]
            right.append(
                jnp.concatenate(
                    [jnp.where(hit, piece[r : r + 1, :], none) for piece in (high, low)], axis=0
                )
            )
        both = lax.dot_general(
            jnp.concatenate(left, axis=1),
            jnp.concatenate(right, axis=1),
            (((1,), (1,)), ((), ())),
            preferred_element_type=F32,
        )
        dense = both[:, :LANES] + both[:, LANES:]
        first = pl.multiple_of((k ^ j) * ny, ny)
        out[pl.ds(first, ny)] = dense.reshape(ny, 8, LANES)
        pot = (src[block + rows : rest, :] - (spectral_center - 3.0)) * (1.0 / spectral_half)
        out[pl.ds(first, ny), slots : slots + 1, :] = pot.reshape(ny, 1, LANES)


def edge_tiles(tile, width, shift):
    lane = lane_iota(tile.shape)
    above = jnp.where(lane < width, pltpu.roll(tile, LANES - shift, 1), 0.0)
    below = jnp.where((lane >= shift) & (lane < shift + width), pltpu.roll(tile, shift, 1), 0.0)
    return above, below


def coef_tile(sums, slots, atom_dev):
    atoms = (GROUP + 2) * atom_dev
    lane = lane_iota((8, LANES))
    tile = jnp.zeros((8, LANES), F32)
    for t in range(atoms):
        total = None
        for p in range(GROUP):
            slot = t - p * atom_dev
            if 0 <= slot < slots:
                total = sums[p][slot] if total is None else total + sums[p][slot]
        tile = jnp.where(lane == t, jnp.sum(total, axis=1, keepdims=True), tile)
    return tile


def relay_kernel(ny, atom_dev, first, idx, *refs):
    slots = 3 * atom_dev
    ins, (dense, field, tile_out, up, down, sums) = refs[:GROUP], refs[GROUP:]
    k = lax.rem(idx[0], GROUP)
    if first:
        fill_dense(ny, slots, k, ins, dense)
    un = 8
    for j in range(GROUP):
        p = k ^ j
        src = ins[j]

        def body(yb, accs, src=src, p=p):
            accs = list(accs)
            for yy in range(un):
                y = yb * un + yy
                v = src[pl.ds(y, 8, stride=ny), :]
                row = p * ny + y
                field[row] = v
                for s in range(slots):
                    accs[s] = accs[s] + v * dense[row, s : s + 1, :]
            return tuple(accs)

        zero = jnp.zeros((8, LANES), F32)
        accs = lax.fori_loop(0, ny // un, body, (zero,) * slots)
        for s in range(slots):
            sums[p * slots + s] = accs[s]
    parts = [[sums[p * slots + s] for s in range(slots)] for p in range(GROUP)]
    tile = coef_tile(parts, slots, atom_dev)
    tile_out[...] = tile
    above, below = edge_tiles(tile, 2 * atom_dev, GROUP * atom_dev)
    up[ny] = above
    down[ny] = below
    up[0:ny] = field[(GROUP - 1) * ny : GROUP * ny]
    down[0:ny] = field[0:ny]


def step_kernel(kind, ny, devices, atoms, *refs):
    atom_dev = atoms // devices
    slots = 3 * atom_dev
    refs = list(refs)
    take = lambda count: [refs.pop(0) for _ in range(count)]
    consts, dense, field, tile_in, below, above = take(6)
    zsum = refs.pop()
    if kind == "b1":
        (other,) = take(1)
    elif kind == "t2":
        other, full_zero, b1, tile_b1, b2, tile_b2, cot, full_cot = take(8)
    elif kind == "out":
        other, cot, gp, e, e_below, e_above = take(6)
    if kind in ("b2", "t1"):
        new, tile_out, up, down, full_out = refs
    elif kind == "b1":
        new, tile_out, up, down = refs
    elif kind == "t2":
        gp, e_out, e_up, e_down = refs
    else:
        (new,) = refs

    full = tile_in[...] + below[ny] + above[ny]
    if kind in ("b2", "t1"):
        full_out[...] = full
    near = (GROUP + 2) * atom_dev
    c0, c1, c2, c3 = [consts[near + n : near + n + 1, :] for n in range(4)]
    keep, scale, mix = {
        "t1": (None, 1.0, None),
        "t2": (None, 2.0, -1.0),
        "b2": (c2, 2.0 * c3, None),
        "b1": (None, 2.0, c1 - c3),
        "out": (None, 1.0, -1.0),
    }[kind]
    spread = []
    for t in range(near):
        coupling = consts[t : t + 1, :] * scale
        spread.append(jnp.broadcast_to(full[:, t : t + 1], (8, LANES)) * coupling)
    side = scale * (-0.5 / spectral_half)
    un = 32
    sums = []
    part = 9 * ny + 8
    lane, line = (lax.broadcasted_iota(jnp.int32, (2 * LANES, LANES), d) for d in (1, 0))
    apart = (lane - line) % LANES
    turn = jnp.where((apart == 1) | (apart == LANES - 1), 1.0, 0.0).astype(jnp.bfloat16)
    for p in range(GROUP):
        flat = field[p * ny : (p + 1) * ny].reshape(8 * ny, LANES)
        high = flat.astype(jnp.bfloat16)
        low = (flat - high.astype(F32)).astype(jnp.bfloat16)
        zsum[p * ny : (p + 1) * ny] = jnp.dot(
            jnp.concatenate([high, low], axis=1), turn, preferred_element_type=F32
        ).reshape(ny, 8, LANES)
    for p in range(GROUP):

        def body(yb, accs, p=p):
            accs = list(accs)
            rows = []
            first = yb * un
            before = p * ny + jnp.where(first == 0, ny - 1, first - 1)
            after = p * ny + jnp.where(first == ny - un, 0, first + un)
            lines = [field[before]] + [field[p * ny + first + yy] for yy in range(un)] + [field[after]]
            for yy in range(un):
                y = first + yy
                row = p * ny + y
                earlier, v, later = lines[yy : yy + 3]
                under = field[row - ny] if p > 0 else below[y]
                over = field[row + ny] if p < GROUP - 1 else above[y]
                beside = (later + earlier) + (under + over)
                beside = beside + zsum[row]
                pot = dense[row, slots : slots + 1, :] * scale
                if keep is not None:
                    pot = pot + keep
                weights = [dense[row, s : s + 1, :] for s in range(slots)]
                a = [spread[p * atom_dev + s] * weights[s] for s in range(slots)]
                while len(a) > 1:
                    a = [sum(a[n : n + 2][1:], a[n]) for n in range(0, len(a), 2)]
                a = a[0]
                x = v * pot + beside * side + a
                if mix is not None:
                    x = x + other[row] * mix
                if kind == "out":
                    x = x + cot[row] * c0
                    new[pl.ds(p * part + y, 8, stride=ny), :] = x
                elif kind == "t2":
                    g = b1[row] * other[row] + 2.0 * (b2[row] * v)
                    g = g + (2.0 * c3) * (cot[row] * x)
                    rows.append(jnp.sum(g, axis=0, keepdims=True))
                else:
                    new[row] = x
                if kind != "out":
                    for s in range(slots):
                        accs[s] = accs[s] + x * weights[s]
            if kind == "t2":
                start = pl.multiple_of(p * ny + yb * un, un)
                gp[pl.ds(start, un), :] = jnp.concatenate(rows, axis=0) * (1.0 / spectral_half)
            return tuple(accs)

        zero = jnp.zeros((8, LANES), F32)
        init = () if kind == "out" else (zero,) * slots
        sums.append(lax.fori_loop(0, ny // un, body, init))
    if kind == "out":
        total = e[...] + e_below[...] + e_above[...]
        for p in range(GROUP):
            rest = p * part + 8 * ny
            new[rest : rest + ny, :] = gp[p * ny : (p + 1) * ny, :]
            new[rest + ny : rest + ny + 8, :] = total
        return
    tile = coef_tile(sums, slots, atom_dev)
    if kind == "t2":
        e = tile_b1[...] * full_zero[...] + 2.0 * (tile_b2[...] * full)
        e = e + (2.0 * c3) * (full_cot[...] * tile)
        e = jnp.sum(e, axis=0, keepdims=True) * (1.0 / spectral_half)
        e = jnp.broadcast_to(e, (8, LANES))
        e_out[...] = e
        lane = lane_iota(e.shape)
        shift = GROUP * atom_dev
        own = (lane >= atom_dev) & (lane < shift + atom_dev)
        e_up[...] = jnp.where(own, pltpu.roll(e, LANES - shift, 1), 0.0)
        e_down[...] = jnp.where(own, pltpu.roll(e, shift, 1), 0.0)
        return
    tile_out[...] = tile
    over, under = edge_tiles(tile, 2 * atom_dev, GROUP * atom_dev)
    up[ny] = over
    down[ny] = under
    up[0:ny] = new[(GROUP - 1) * ny : GROUP * ny]
    down[0:ny] = new[0:ny]


def final_kernel(ny, atom_dev, idx, *refs):
    blocks, (out, gp_out, e_out, gp, sems) = refs[:GROUP], refs[GROUP:]
    k = lax.rem(idx[0], GROUP)
    rows = 8 * ny
    copies, parts = [], []
    for j in range(GROUP):
        start = pl.multiple_of(k * (rows + ny + 8), 8) if j == 0 else 0
        first = pl.multiple_of((k ^ j) * rows, rows)
        copies.append(
            pltpu.make_async_copy(
                blocks[j].at[pl.ds(start, rows)], out.at[pl.ds(first, rows)], sems.at[j]
            )
        )
        parts.append(blocks[j][pl.ds(start + rows, ny + 8), :])
    for copy in copies:
        copy.start()
    total = (parts[0] + parts[1]) + (parts[2] + parts[3])
    gp[...] = total[0:ny]
    last = pltpu.make_async_copy(gp, gp_out, sems.at[GROUP])
    last.start()
    e = total[ny : ny + 1]
    lane = lane_iota(e.shape)
    for n in range(atom_dev):
        e_out[n] = jnp.sum(jnp.where(lane == (k + 1) * atom_dev + n, e, 0.0))
    for copy in copies + [last]:
        copy.wait()


def per_device(orbitals, cotangent, potential, cheb_coef, energy, proj_cell, proj_atom, proj_value):
    orb, _, ny, nz = orbitals.shape
    devices = lax.axis_size("grid")
    slabs = devices // GROUP
    atoms = energy.shape[0]
    atom_dev = atoms // devices
    points = proj_cell.shape[0] // LANES
    assert orb == 8 * GROUP and nz == LANES and devices % GROUP == 0
    idx = lax.axis_index("grid").astype(jnp.int32).reshape(1)
    block = 8 * ny
    plane = GROUP * ny

    def near(x, j):
        return lax.ppermute(x, "grid", [(a, a ^ j) for a in range(devices)])

    to_above = [
        (GROUP * s + m, GROUP * ((s + 1) % slabs) + m) for s in range(slabs) for m in range(GROUP)
    ]
    to_below = [(b, a) for a, b in to_above]

    def halo(up, down):
        return lax.ppermute(up, "grid", to_above), lax.ppermute(down, "grid", to_below)

    def gather(blocks):
        return [blocks[0]] + [near(blocks[j], j) for j in range(1, GROUP)]

    consts, *blocks = call(
        functools.partial(prep_kernel, devices, atoms),
        [(-(-(GROUP * atom_dev + 2 * atom_dev + 4) // 8) * 8, LANES)]
        + [(block + 3 * points + ny, LANES)] * GROUP
        + [(block, LANES)] * GROUP,
        idx,
        cheb_coef,
        energy,
        proj_cell.reshape(points, LANES),
        proj_atom.reshape(points, LANES),
        proj_value.reshape(points, LANES),
        potential.reshape(ny, LANES),
        cotangent.reshape(orb * ny, LANES),
        orbitals.reshape(orb * ny, LANES),
        micros=1.2,
        scratch=[
            pltpu.VMEM((2, points, LANES), jnp.int32),
            pltpu.SemaphoreType.DMA((4 * GROUP,)),
            pltpu.SemaphoreType.DMA((2,)),
        ],
        smem=(0, 1, 2),
        hbm_args=(3, 4, 5, 6, 7, 8),
    )
    cot_blocks = gather(blocks[:GROUP])
    orb_blocks = gather(blocks[GROUP:])
    field_shape, tile_shape, edge_shape = (plane, 8, LANES), (8, LANES), (ny + 1, 8, LANES)
    chain = [field_shape, tile_shape, edge_shape, edge_shape]

    def relay(first, blocks, *args):
        return call(
            functools.partial(relay_kernel, ny, atom_dev, first),
            ([field_shape] if first else []) + chain,
            idx,
            *blocks,
            *args,
            micros=2.0 if first else 0.7,
            scratch=[pltpu.VMEM((GROUP * 3 * atom_dev, 8, LANES), F32)],
            smem=(0,),
        )

    def step(kind, outs, *args):
        return call(
            functools.partial(step_kernel, kind, ny, devices, atoms),
            outs,
            consts,
            dense,
            *args,
            micros=1.5,
            scratch=[pltpu.VMEM(field_shape, F32)],
        )

    dense, cot, tile_cot, up, down = relay(True, cot_blocks)
    cot_halo = halo(up, down)
    zero, tile_zero, up, down = relay(False, orb_blocks, dense)
    zero_halo = halo(up, down)
    b2, tile_b2, up, down, full_cot = step("b2", chain + [tile_shape], cot, tile_cot, *cot_halo)
    b2_halo = halo(up, down)
    t1, tile_t1, up, down, full_zero = step("t1", chain + [tile_shape], zero, tile_zero, *zero_halo)
    t1_halo = halo(up, down)
    b1, tile_b1, up, down = step("b1", chain, b2, tile_b2, *b2_halo, cot)
    b1_halo = halo(up, down)
    gp, e, e_up, e_down = step(
        "t2",
        [(plane, LANES)] + [tile_shape] * 3,
        t1,
        tile_t1,
        *t1_halo,
        zero,
        full_zero,
        b1,
        tile_b1,
        b2,
        tile_b2,
        cot,
        full_cot,
    )
    (image,) = step(
        "out",
        [(GROUP * (block + ny + 8), LANES)],
        b1,
        tile_b1,
        *b1_halo,
        b2,
        cot,
        gp,
        e,
        *halo(e_up, e_down),
    )
    member, part = lax.rem(idx[0], GROUP), block + ny + 8
    images = [image] + [
        near(lax.dynamic_slice_in_dim(image, (member ^ j) * part, part, 0), j)
        for j in range(1, GROUP)
    ]
    out, gp, e = call(
        functools.partial(final_kernel, ny, atom_dev),
        [(orb * ny, LANES), (ny, LANES), (atom_dev,)],
        idx,
        *images,
        micros=1.0,
        scratch=[pltpu.VMEM((ny, LANES), F32), pltpu.SemaphoreType.DMA((GROUP + 1,))],
        smem=(0,),
        hbm_outs=(0, 1),
        smem_outs=(2,),
    )
    return out.reshape(orbitals.shape), gp.reshape(potential.shape), e


def solution(mesh):
    placed = (
        P("sample", "grid", None, None),
        P("sample", "grid", None, None),
        P("grid", None, None),
        P(),
        P(),
        P("grid"),
        P("grid"),
        P("grid"),
    )
    return jax.shard_map(
        per_device,
        mesh=mesh,
        in_specs=placed,
        out_specs=(
            P("sample", "grid", None, None),
            P(("sample", "grid"), None, None),
            P(("sample", "grid")),
        ),
        check_vma=False,
    )
```

```python
import functools

import jax
import jax.numpy as jnp
from jax import lax
from jax.experimental import pallas as pl
from jax.experimental.pallas import tpu as pltpu
from jax.sharding import PartitionSpec as P

spectral_center = 4.5
spectral_half = 4.5

GROUP = 4
SLAB = 2
NEAR = SLAB + 2
LANES = 128
F32 = jnp.float32


def call(body, outs, *args, micros, scratch=(), smem=(), hbm_args=(), hbm_outs=(), smem_outs=()):
    in_specs, operands = [], []
    for n, a in enumerate(args):
        if n in smem:
            in_specs.append(pl.BlockSpec(memory_space=pltpu.SMEM))
        elif n in hbm_args:
            in_specs.append(pl.BlockSpec(memory_space=pltpu.HBM))
            a = pltpu.with_memory_space_constraint(a, pltpu.HBM)
        else:
            in_specs.append(pl.BlockSpec(memory_space=pltpu.VMEM))
            a = pltpu.with_memory_space_constraint(a, pltpu.VMEM)
        operands.append(a)
    out_shape, out_specs = [], []
    for n, shape in enumerate(outs):
        if n in hbm_outs:
            out_shape.append(jax.ShapeDtypeStruct(shape, F32))
            out_specs.append(pl.BlockSpec(memory_space=pltpu.HBM))
        elif n in smem_outs:
            out_shape.append(jax.ShapeDtypeStruct(shape, F32))
            out_specs.append(pl.BlockSpec(memory_space=pltpu.SMEM))
        else:
            out_shape.append(pltpu.VMEM(shape, F32))
            out_specs.append(pl.BlockSpec(memory_space=pltpu.VMEM))
    return pl.pallas_call(
        body,
        out_shape=out_shape,
        in_specs=in_specs,
        out_specs=out_specs,
        scratch_shapes=list(scratch),
        compiler_params=pltpu.CompilerParams(vmem_limit_bytes=16 << 20),
        cost_estimate=pl.CostEstimate(
            flops=int(micros * 1e6), bytes_accessed=int(micros * 3.69e6), transcendentals=0
        ),
    )(*operands)


def lane_iota(shape):
    return lax.broadcasted_iota(jnp.int32, shape, len(shape) - 1)


def prep_kernel(devices, atoms, idx, cheb, energy, cell, atom, value, pot, cot, *refs):
    consts, blocks = refs[0], refs[1:3]
    box, cheb_box, energy_box, value_box, pot_box, sems = refs[3:]
    count, ny = cell.shape[0], pot.shape[0]
    rows = blocks[0].shape[0] - 3 * count - ny
    atom_dev = atoms // devices
    k = lax.rem(idx[0], GROUP)
    moves = [(cell, box.at[0]), (atom, box.at[1]), (cheb, cheb_box), (energy, energy_box)]
    moves += [(value, value_box), (pot, pot_box)]
    for n in range(2):
        first = pl.multiple_of((lax.rem(k, 2) ^ (1 - n)) * rows, rows)
        moves.append((cot.at[pl.ds(first, rows)], blocks[n].at[pl.ds(0, rows)]))
    copies = [
        pltpu.make_async_copy(src, dst, sems.at[n]) for n, (src, dst) in enumerate(moves)
    ]
    for copy in copies[::-1]:
        copy.start()
    for copy in copies[:6]:
        copy.wait()
    up = lax.rem(k, 2) == 1
    first_plane = idx[0] - k + lax.rem(k, 2) * SLAB - 1
    for t in range(NEAR * atom_dev):
        h, r = t // atom_dev, t % atom_dev
        a = (first_plane + jnp.where(up, h, NEAR - 1 - h)) * atom_dev + r
        a = jnp.where(a < 0, a + atoms, jnp.where(a >= atoms, a - atoms, a))
        consts[t : t + 1, :] = jnp.full((1, LANES), energy_box[a] * (1.0 / spectral_half), F32)
    for n in range(4):
        at = NEAR * atom_dev + n
        consts[at : at + 1, :] = jnp.full((1, LANES), cheb_box[n], F32)
    shifted = box[1] + (atoms - (idx[0] - 1) * atom_dev)
    shifted = jnp.where(shifted >= 2 * atoms, shifted - 2 * atoms, shifted)
    slot = jnp.where(shifted >= atoms, shifted - atoms, shifted)
    home = jnp.where(slot >= 2 * atom_dev, 2, jnp.where(slot >= atom_dev, 1, 0))
    slot = jnp.where(k >= 2, slot, slot + (2 - 2 * home) * atom_dev)
    for block in blocks:
        at = rows
        for part in (value_box[...], pot_box[...], box[0].astype(F32), slot.astype(F32)):
            block[at : at + part.shape[0], :] = part
            at += part.shape[0]
    for copy in copies[6:]:
        copy.wait()


def pack_kernel(idx, field, *refs):
    blocks, sems = refs[:2], refs[2]
    rows = blocks[0].shape[0]
    k = lax.rem(idx[0], GROUP)
    copies = []
    for n in range(2):
        first = pl.multiple_of((lax.rem(k, 2) ^ (1 - n)) * rows, rows)
        copies.append(
            pltpu.make_async_copy(field.at[pl.ds(first, rows)], blocks[n], sems.at[n])
        )
    for copy in copies:
        copy.start()
    for copy in copies:
        copy.wait()


def first_place(k):
    return jnp.where((k == 1) | (k == 2), 1, 0)


def fill_dense(ny, slots, block, places, ins, out):
    rows = (ins[0].shape[0] - block - ny) // 3
    rest = block + rows + ny
    half = jnp.bfloat16
    place = lax.broadcasted_iota(jnp.int32, (ny * 8, LANES), 0).astype(F32).astype(half)
    column = lax.broadcasted_iota(jnp.int32, (LANES, LANES), 0).astype(F32).astype(half)
    one, none = jnp.ones((), half), jnp.zeros((), half)
    for p, src in zip(places, ins):
        cell = src[rest : rest + rows, :]
        line = jnp.floor(cell * (1.0 / LANES))
        z = (cell - line * LANES).astype(half)
        code = (line * 8 + src[rest + rows : rest + 2 * rows, :]).astype(half)
        value = src[block : block + rows, :]
        high = value.astype(half)
        low = (value - high.astype(F32)).astype(half)
        left, right = [], []
        for r in range(rows):
            left.append(jnp.where(place == code[r : r + 1, :], one, none))
            hit = column == z[r : r + 1, :]
            right.append(
                jnp.concatenate(
                    [jnp.where(hit, piece[r : r + 1, :], none) for piece in (high, low)], axis=0
                )
            )
        both = lax.dot_general(
            jnp.concatenate(left, axis=1),
            jnp.concatenate(right, axis=1),
            (((1,), (1,)), ((), ())),
            preferred_element_type=F32,
        )
        dense = both[:, :LANES] + both[:, LANES:]
        first = pl.multiple_of(p * ny, ny)
        out[pl.ds(first, ny)] = dense.reshape(ny, 8, LANES)
        pot = (src[block + rows : rest, :] - (spectral_center - 3.0)) * (1.0 / spectral_half)
        out[pl.ds(first, ny), slots : slots + 1, :] = pot.reshape(ny, 1, LANES)


def edge_tiles(tile, atom_dev):
    lane = lane_iota(tile.shape)
    earlier, later = pltpu.roll(tile, atom_dev, 1), pltpu.roll(tile, LANES - atom_dev, 1)
    turned = jnp.where(lax.rem(lane, 2 * atom_dev) < atom_dev, later, earlier)
    inner = jnp.where(lane < 2 * atom_dev, turned, 0.0)
    outer = jnp.where((lane >= 2 * atom_dev) & (lane < 4 * atom_dev), turned, 0.0)
    return inner, outer


def coef_tile(sums, slots, atom_dev):
    shape = sums[0][0].shape
    lane = lane_iota(shape)
    tile = jnp.zeros(shape, F32)
    for t in range(NEAR * atom_dev):
        total = None
        for p in range(SLAB):
            slot = t - p * atom_dev
            if 0 <= slot < slots:
                total = sums[p][slot] if total is None else total + sums[p][slot]
        tile = jnp.where(lane == t, jnp.sum(total, axis=1, keepdims=True), tile)
    return tile


def put_edges(ny, atom_dev, field, tile, inner, outer):
    inner[ny], outer[ny] = edge_tiles(tile, atom_dev)
    inner[0:ny] = field[0:ny]
    outer[0:ny] = field[ny : 2 * ny]


def relay_kernel(ny, orb, atom_dev, first, idx, *refs):
    slots = 3 * atom_dev
    ins, (dense, field, tile_out, inner, outer, sums) = refs[:2], refs[2:]
    place = first_place(lax.rem(idx[0], GROUP))
    places = (place, 1 - place)
    if first:
        fill_dense(ny, slots, orb * ny, places, ins, dense)
    un = 8
    for p, src in zip(places, ins):

        def body(yb, accs, src=src, p=p):
            accs = list(accs)
            for yy in range(un):
                y = yb * un + yy
                v = src[pl.ds(y, orb, stride=ny), :]
                row = p * ny + y
                field[row] = v
                for s in range(slots):
                    accs[s] = accs[s] + v * dense[row, s : s + 1, :]
            return tuple(accs)

        zero = jnp.zeros((orb, LANES), F32)
        accs = lax.fori_loop(0, ny // un, body, (zero,) * slots)
        for s in range(slots):
            sums[p * slots + s] = accs[s]
    parts = [[sums[p * slots + s] for s in range(slots)] for p in range(SLAB)]
    tile = coef_tile(parts, slots, atom_dev)
    tile_out[...] = tile
    put_edges(ny, atom_dev, field, tile, inner, outer)


def step_kernel(kind, ny, atom_dev, *refs):
    slots = 3 * atom_dev
    refs = list(refs)
    zsum = refs.pop()
    take = lambda count: [refs.pop(0) for _ in range(count)]
    consts, dense, field, tile_in, inside, outside = take(6)
    if kind == "b1":
        (other,) = take(1)
    elif kind == "t2":
        other, full_zero, b1, tile_b1, b2, tile_b2, cot, full_cot = take(8)
    elif kind == "out":
        other, cot, gp, e, e_inside, e_outside = take(6)
    if kind in ("b2", "t1"):
        new, tile_out, inner, outer, full_out = refs
    elif kind == "b1":
        new, tile_out, inner, outer = refs
    elif kind == "t2":
        gp, e_out, e_inner, e_outer = refs
    else:
        (new,) = refs
    orb = field.shape[1]
    full = tile_in[...] + inside[ny] + outside[ny]
    if kind in ("b2", "t1"):
        full_out[...] = full
    near = NEAR * atom_dev
    c0, c1, c2, c3 = [consts[near + n : near + n + 1, :] for n in range(4)]
    keep, scale, mix = {
        "t1": (None, 1.0, None),
        "t2": (None, 2.0, -1.0),
        "b2": (c2, 2.0 * c3, None),
        "b1": (None, 2.0, c1 - c3),
        "out": (None, 1.0, -1.0),
    }[kind]
    spread = []
    for t in range(near):
        coupling = consts[t : t + 1, :] * scale
        spread.append(jnp.broadcast_to(full[:, t : t + 1], (orb, LANES)) * coupling)
    side = scale * (-0.5 / spectral_half)
    sums = []
    part = (orb + 1) * ny + 8
    lane, line = (lax.broadcasted_iota(jnp.int32, (2 * LANES, LANES), d) for d in (1, 0))
    apart = (lane - line) % LANES
    turn = jnp.where((apart == 1) | (apart == LANES - 1), 1.0, 0.0).astype(jnp.bfloat16)
    for p in range(SLAB):
        flat = field[p * ny : (p + 1) * ny].reshape(orb * ny, LANES)
        high = flat.astype(jnp.bfloat16)
        low = (flat - high.astype(F32)).astype(jnp.bfloat16)
        zsum[p * ny : (p + 1) * ny] = jnp.dot(
            jnp.concatenate([high, low], axis=1), turn, preferred_element_type=F32
        ).reshape(ny, orb, LANES)
    un = ny
    for p in range(SLAB):

        def body(yb, accs, p=p):
            accs = list(accs)
            rows = []
            first = yb * un
            before = p * ny + jnp.where(first == 0, ny - 1, first - 1)
            after = p * ny + jnp.where(first == ny - un, 0, first + un)
            lines = [field[before]] + [field[p * ny + first + yy] for yy in range(un)]
            lines.append(field[after])
            for yy in range(un):
                y = first + yy
                row = p * ny + y
                earlier, v, later = lines[yy : yy + 3]
                beyond = (outside if p else inside)[y] + field[(1 - p) * ny + y]
                beside = (later + earlier) + (beyond + zsum[row])
                pot = dense[row, slots : slots + 1, :] * scale
                if keep is not None:
                    pot = pot + keep
                weights = [dense[row, s : s + 1, :] for s in range(slots)]
                a = [spread[p * atom_dev + s] * weights[s] for s in range(slots)]
                while len(a) > 1:
                    a = [sum(a[n + 1 : n + 2], a[n]) for n in range(0, len(a), 2)]
                x = v * pot + beside * side + a[0]
                if mix is not None:
                    x = x + other[row] * mix
                if kind == "out":
                    x = x + cot[row] * c0
                    new[pl.ds(p * part + y, orb, stride=ny), :] = x
                elif kind == "t2":
                    g = b1[row] * other[row] + 2.0 * (b2[row] * v)
                    g = g + (2.0 * c3) * (cot[row] * x)
                    rows.append(jnp.sum(g, axis=0, keepdims=True))
                else:
                    new[row] = x
                if kind != "out":
                    for s in range(slots):
                        accs[s] = accs[s] + x * weights[s]
            if kind == "t2":
                start = pl.multiple_of(p * ny + yb * un, un)
                gp[pl.ds(start, un), :] = jnp.concatenate(rows, axis=0) * (1.0 / spectral_half)
            return tuple(accs)

        zero = jnp.zeros((orb, LANES), F32)
        init = () if kind == "out" else (zero,) * slots
        sums.append(lax.fori_loop(0, ny // un, body, init))
    if kind == "out":
        total = e[...] + e_inside[...] + e_outside[...]
        for p in range(SLAB):
            rest = p * part + orb * ny
            new[rest : rest + ny, :] = gp[p * ny : (p + 1) * ny, :]
            new[rest + ny : rest + ny + 8, :] = pltpu.roll(total, LANES - (p + 1) * atom_dev, 1)
        return
    tile = coef_tile(sums, slots, atom_dev)
    if kind == "t2":
        e = tile_b1[...] * full_zero[...] + 2.0 * (tile_b2[...] * full)
        e = e + (2.0 * c3) * (full_cot[...] * tile)
        e = jnp.sum(e, axis=0, keepdims=True) * (1.0 / spectral_half)
        e = jnp.broadcast_to(e, (8, LANES))
        e_out[...] = e
        lane = lane_iota(e.shape)
        mine = (lane >= atom_dev) & (lane < 2 * atom_dev)
        e_inner[...] = jnp.where(mine, pltpu.roll(e, atom_dev, 1), 0.0)
        mine = (lane >= 2 * atom_dev) & (lane < 3 * atom_dev)
        e_outer[...] = jnp.where(mine, pltpu.roll(e, LANES - atom_dev, 1), 0.0)
        return
    tile_out[...] = tile
    put_edges(ny, atom_dev, new, tile, inner, outer)


def final_kernel(ny, orb, atom_dev, idx, *refs):
    blocks, (out, gp_out, e_out, gp, sems) = refs[:2], refs[2:]
    k = lax.rem(idx[0], GROUP)
    rows = orb * ny
    copies = []
    for n in range(2):
        first = pl.multiple_of((lax.rem(k, 2) ^ (1 - n)) * rows, rows)
        copies.append(
            pltpu.make_async_copy(
                blocks[n].at[pl.ds(0, rows)], out.at[pl.ds(first, rows)], sems.at[n]
            )
        )
    for copy in copies:
        copy.start()
    total = blocks[0][rows:, :] + blocks[1][rows:, :]
    gp[...] = total[0:ny]
    last = pltpu.make_async_copy(gp, gp_out, sems.at[2])
    last.start()
    e = total[ny : ny + 1]
    lane = lane_iota(e.shape)
    for n in range(atom_dev):
        e_out[n] = jnp.sum(jnp.where(lane == n, e, 0.0))
    for copy in copies + [last]:
        copy.wait()


def per_device(orbitals, cotangent, potential, cheb_coef, energy, proj_cell, proj_atom, proj_value):
    orb_all, _, ny, nz = orbitals.shape
    devices = lax.axis_size("grid")
    groups = devices // GROUP
    atoms = energy.shape[0]
    atom_dev = atoms // devices
    points = proj_cell.shape[0] // LANES
    orb = orb_all // 2
    assert orb % 8 == 0 and nz == LANES and devices % GROUP == 0
    idx = lax.axis_index("grid").astype(jnp.int32).reshape(1)
    block = orb * ny
    plane = SLAB * ny

    def pairs(within):
        return [(GROUP * g + a, GROUP * g + b) for g in range(groups) for a, b in within]

    enter = [(0, 2), (1, 0), (2, 3), (3, 1)]
    leave = [(b, a) for a, b in enter]
    swap = [(0, 0), (1, 2), (2, 1), (3, 3)]
    core = pairs([(0, 1), (1, 0), (2, 3), (3, 2)])
    across = []
    for g in range(groups):
        for m in range(2):
            below, above = GROUP * g + 2 * m + 1, GROUP * ((g + 1) % groups) + 2 * m
            across += [(below, above), (above, below)]

    def permute(x, to):
        return lax.ppermute(x, "grid", to)

    def halo(inner, outer):
        beyond = permute(outer, across)
        return permute(inner, core), beyond

    def exchange(blocks, first):
        return [permute(blocks[0], pairs(first)), permute(blocks[1], pairs(swap))]

    consts, *blocks = call(
        functools.partial(prep_kernel, devices, atoms),
        [(-(-(NEAR * atom_dev + 4) // 8) * 8, LANES)] + [(block + 3 * points + ny, LANES)] * 2,
        idx,
        cheb_coef,
        energy,
        proj_cell.reshape(points, LANES),
        proj_atom.reshape(points, LANES),
        proj_value.reshape(points, LANES),
        potential.reshape(ny, LANES),
        cotangent.reshape(orb_all * ny, LANES),
        micros=1.2,
        scratch=[
            pltpu.VMEM((2, points, LANES), jnp.int32),
            pltpu.SMEM(cheb_coef.shape, F32),
            pltpu.SMEM(energy.shape, F32),
            pltpu.VMEM((points, LANES), F32),
            pltpu.VMEM((ny, LANES), F32),
            pltpu.SemaphoreType.DMA((8,)),
        ],
        smem=(0,),
        hbm_args=range(1, 8),
    )
    cot_blocks = exchange(blocks, enter)
    blocks = call(
        pack_kernel,
        [(block, LANES)] * 2,
        idx,
        orbitals.reshape(orb_all * ny, LANES),
        micros=1.0,
        scratch=[pltpu.SemaphoreType.DMA((2,))],
        smem=(0,),
        hbm_args=(1,),
    )
    orb_blocks = exchange(blocks, enter)
    field_shape, tile_shape = (plane, orb, LANES), (orb, LANES)
    edge_shape, sums_shape = (ny + 1, orb, LANES), (8, LANES)
    chain = [field_shape, tile_shape, edge_shape, edge_shape]

    def relay(first, blocks, *args):
        return call(
            functools.partial(relay_kernel, ny, orb, atom_dev, first),
            ([(plane, 8, LANES)] if first else []) + chain,
            idx,
            *blocks,
            *args,
            micros=1.4 if first else 0.7,
            scratch=[pltpu.VMEM((SLAB * 3 * atom_dev, orb, LANES), F32)],
            smem=(0,),
        )

    def step(kind, outs, *args):
        return call(
            functools.partial(step_kernel, kind, ny, atom_dev),
            outs,
            consts,
            dense,
            *args,
            micros=1.0,
            scratch=[pltpu.VMEM(field_shape, F32)],
        )

    dense, cot, tile_cot, *edges = relay(True, cot_blocks)
    inner, outer = edges
    cot_halo = halo(inner, outer)
    cot_halo = (
        cot_halo[0],
        jnp.concatenate([permute(outer[:ny], across), permute(outer[ny:], across)]),
    )
    zero, tile_zero, *edges = relay(False, orb_blocks, dense)
    zero_halo = halo(*edges)
    b2, tile_b2, *edges, full_cot = step("b2", chain + [tile_shape], cot, tile_cot, *cot_halo)
    b2_halo = halo(*edges)
    t1, tile_t1, *edges, full_zero = step("t1", chain + [tile_shape], zero, tile_zero, *zero_halo)
    t1_halo = halo(*edges)
    b1, tile_b1, *edges = step("b1", chain, b2, tile_b2, *b2_halo, cot)
    b1_halo = halo(*edges)
    gp, e, *edges = step(
        "t2",
        [(plane, LANES)] + [sums_shape] * 3,
        t1,
        tile_t1,
        *t1_halo,
        zero,
        full_zero,
        b1,
        tile_b1,
        b2,
        tile_b2,
        cot,
        full_cot,
    )
    part = block + ny + 8
    (image,) = step(
        "out", [(SLAB * part, LANES)], b1, tile_b1, *b1_halo, b2, cot, gp, e, *halo(*edges)
    )
    place = first_place(lax.rem(idx[0], GROUP))
    images = exchange(
        [
            lax.dynamic_slice_in_dim(image, place * part, part, 0),
            lax.dynamic_slice_in_dim(image, (1 - place) * part, part, 0),
        ],
        leave,
    )
    out, gp, e = call(
        functools.partial(final_kernel, ny, orb, atom_dev),
        [(orb_all * ny, LANES), (ny, LANES), (atom_dev,)],
        idx,
        *images,
        micros=1.0,
        scratch=[pltpu.VMEM((ny, LANES), F32), pltpu.SemaphoreType.DMA((3,))],
        smem=(0,),
        hbm_outs=(0, 1),
        smem_outs=(2,),
    )
    return out.reshape(orbitals.shape), gp.reshape(potential.shape), e


def solution(mesh):
    placed = (
        P("sample", "grid", None, None),
        P("sample", "grid", None, None),
        P("grid", None, None),
        P(),
        P(),
        P("grid"),
        P("grid"),
        P("grid"),
    )
    return jax.shard_map(
        per_device,
        mesh=mesh,
        in_specs=placed,
        out_specs=(
            P("sample", "grid", None, None),
            P(("sample", "grid"), None, None),
            P(("sample", "grid")),
        ),
        check_vma=False,
    )
```

```python
import functools

import jax
import jax.numpy as jnp
from jax import lax
from jax.experimental import pallas as pl
from jax.experimental.pallas import tpu as pltpu
from jax.sharding import PartitionSpec as P

spectral_center = 4.5
spectral_half = 4.5

GROUP = 4
SLAB = 2
NEAR = SLAB + 2
LANES = 128
F32 = jnp.float32


def call(body, outs, *args, micros, scratch=(), smem=(), hbm_args=(), hbm_outs=(), smem_outs=()):
    in_specs, operands = [], []
    for n, a in enumerate(args):
        if n in smem:
            in_specs.append(pl.BlockSpec(memory_space=pltpu.SMEM))
        elif n in hbm_args:
            in_specs.append(pl.BlockSpec(memory_space=pltpu.HBM))
            a = pltpu.with_memory_space_constraint(a, pltpu.HBM)
        else:
            in_specs.append(pl.BlockSpec(memory_space=pltpu.VMEM))
            a = pltpu.with_memory_space_constraint(a, pltpu.VMEM)
        operands.append(a)
    out_shape, out_specs = [], []
    for n, shape in enumerate(outs):
        if n in hbm_outs:
            out_shape.append(jax.ShapeDtypeStruct(shape, F32))
            out_specs.append(pl.BlockSpec(memory_space=pltpu.HBM))
        elif n in smem_outs:
            out_shape.append(jax.ShapeDtypeStruct(shape, F32))
            out_specs.append(pl.BlockSpec(memory_space=pltpu.SMEM))
        else:
            out_shape.append(pltpu.VMEM(shape, F32))
            out_specs.append(pl.BlockSpec(memory_space=pltpu.VMEM))
    return pl.pallas_call(
        body,
        out_shape=out_shape,
        in_specs=in_specs,
        out_specs=out_specs,
        scratch_shapes=list(scratch),
        compiler_params=pltpu.CompilerParams(vmem_limit_bytes=16 << 20),
        cost_estimate=pl.CostEstimate(
            flops=int(micros * 1e6), bytes_accessed=int(micros * 3.69e6), transcendentals=0
        ),
    )(*operands)


def lane_iota(shape):
    return lax.broadcasted_iota(jnp.int32, shape, len(shape) - 1)


def prep_kernel(devices, atoms, idx, cheb, energy, cell, atom, value, pot, cot, *refs):
    consts, blocks = refs[0], refs[1:3]
    box, cheb_box, energy_box, value_box, pot_box, sems = refs[3:]
    count, ny = cell.shape[0], pot.shape[0]
    rows = blocks[0].shape[0] - 3 * count - ny
    atom_dev = atoms // devices
    k = lax.rem(idx[0], GROUP)
    moves = [(cell, box.at[0]), (atom, box.at[1]), (cheb, cheb_box), (energy, energy_box)]
    moves += [(value, value_box), (pot, pot_box)]
    for n in range(2):
        first = pl.multiple_of((lax.rem(k, 2) ^ (1 - n)) * rows, rows)
        moves.append((cot.at[pl.ds(first, rows)], blocks[n].at[pl.ds(0, rows)]))
    copies = [
        pltpu.make_async_copy(src, dst, sems.at[n]) for n, (src, dst) in enumerate(moves)
    ]
    for copy in copies[::-1]:
        copy.start()
    for copy in copies[:6]:
        copy.wait()
    up = lax.rem(k, 2) == 1
    first_plane = idx[0] - k + lax.rem(k, 2) * SLAB - 1
    for t in range(NEAR * atom_dev):
        h, r = t // atom_dev, t % atom_dev
        a = (first_plane + jnp.where(up, h, NEAR - 1 - h)) * atom_dev + r
        a = jnp.where(a < 0, a + atoms, jnp.where(a >= atoms, a - atoms, a))
        consts[t : t + 1, :] = jnp.full((1, LANES), energy_box[a] * (1.0 / spectral_half), F32)
    for n in range(4):
        at = NEAR * atom_dev + n
        consts[at : at + 1, :] = jnp.full((1, LANES), cheb_box[n], F32)
    shifted = box[1] + (atoms - (idx[0] - 1) * atom_dev)
    shifted = jnp.where(shifted >= 2 * atoms, shifted - 2 * atoms, shifted)
    slot = jnp.where(shifted >= atoms, shifted - atoms, shifted)
    home = jnp.where(slot >= 2 * atom_dev, 2, jnp.where(slot >= atom_dev, 1, 0))
    slot = jnp.where(k >= 2, slot, slot + (2 - 2 * home) * atom_dev)
    for block in blocks:
        at = rows
        for part in (value_box[...], pot_box[...], box[0].astype(F32), slot.astype(F32)):
            block[at : at + part.shape[0], :] = part
            at += part.shape[0]
    for copy in copies[6:]:
        copy.wait()


def pack_kernel(idx, field, *refs):
    blocks, sems = refs[:2], refs[2]
    rows = blocks[0].shape[0]
    k = lax.rem(idx[0], GROUP)
    copies = []
    for n in range(2):
        first = pl.multiple_of((lax.rem(k, 2) ^ (1 - n)) * rows, rows)
        copies.append(
            pltpu.make_async_copy(field.at[pl.ds(first, rows)], blocks[n], sems.at[n])
        )
    for copy in copies:
        copy.start()
    for copy in copies:
        copy.wait()


def first_place(k):
    return jnp.where((k == 1) | (k == 2), 1, 0)


def fill_dense(ny, slots, block, places, ins, out):
    rows = (ins[0].shape[0] - block - ny) // 3
    rest = block + rows + ny
    half = jnp.bfloat16
    place = lax.broadcasted_iota(jnp.int32, (ny * 8, LANES), 0).astype(F32).astype(half)
    column = lax.broadcasted_iota(jnp.int32, (LANES, LANES), 0).astype(F32).astype(half)
    one, none = jnp.ones((), half), jnp.zeros((), half)
    for p, src in zip(places, ins):
        cell = src[rest : rest + rows, :]
        line = jnp.floor(cell * (1.0 / LANES))
        z = (cell - line * LANES).astype(half)
        code = (line * 8 + src[rest + rows : rest + 2 * rows, :]).astype(half)
        value = src[block : block + rows, :]
        high = value.astype(half)
        low = (value - high.astype(F32)).astype(half)
        left, right = [], []
        for r in range(rows):
            left.append(jnp.where(place == code[r : r + 1, :], one, none))
            hit = column == z[r : r + 1, :]
            right.append(
                jnp.concatenate(
                    [jnp.where(hit, piece[r : r + 1, :], none) for piece in (high, low)], axis=0
                )
            )
        both = lax.dot_general(
            jnp.concatenate(left, axis=1),
            jnp.concatenate(right, axis=1),
            (((1,), (1,)), ((), ())),
            preferred_element_type=F32,
        )
        dense = both[:, :LANES] + both[:, LANES:]
        first = pl.multiple_of(p * ny, ny)
        out[pl.ds(first, ny)] = dense.reshape(ny, 8, LANES)
        pot = (src[block + rows : rest, :] - (spectral_center - 3.0)) * (1.0 / spectral_half)
        out[pl.ds(first, ny), slots : slots + 1, :] = pot.reshape(ny, 1, LANES)


def edge_tiles(tile, atom_dev):
    lane = lane_iota(tile.shape)
    earlier, later = pltpu.roll(tile, atom_dev, 1), pltpu.roll(tile, LANES - atom_dev, 1)
    turned = jnp.where(lax.rem(lane, 2 * atom_dev) < atom_dev, later, earlier)
    inner = jnp.where(lane < 2 * atom_dev, turned, 0.0)
    outer = jnp.where((lane >= 2 * atom_dev) & (lane < 4 * atom_dev), turned, 0.0)
    return inner, outer


def coef_tile(sums, slots, atom_dev):
    shape = sums[0][0].shape
    lane = lane_iota(shape)
    tile = jnp.zeros(shape, F32)
    for t in range(NEAR * atom_dev):
        total = None
        for p in range(SLAB):
            slot = t - p * atom_dev
            if 0 <= slot < slots:
                total = sums[p][slot] if total is None else total + sums[p][slot]
        tile = jnp.where(lane == t, jnp.sum(total, axis=1, keepdims=True), tile)
    return tile


def put_edges(ny, atom_dev, field, tile, inner, outer):
    inner[ny], outer[ny] = edge_tiles(tile, atom_dev)
    inner[0:ny] = field[0:ny]
    outer[0:ny] = field[ny : 2 * ny]


def relay_kernel(ny, orb, atom_dev, first, idx, *refs):
    slots = 3 * atom_dev
    ins, (dense, field, tile_out, inner, outer, sums) = refs[:2], refs[2:]
    place = first_place(lax.rem(idx[0], GROUP))
    places = (place, 1 - place)
    if first:
        fill_dense(ny, slots, orb * ny, places, ins, dense)
    un = 8
    for p, src in zip(places, ins):

        def body(yb, accs, src=src, p=p):
            accs = list(accs)
            for yy in range(un):
                y = yb * un + yy
                v = src[pl.ds(y, orb, stride=ny), :]
                row = p * ny + y
                field[row] = v
                for s in range(slots):
                    accs[s] = accs[s] + v * dense[row, s : s + 1, :]
            return tuple(accs)

        zero = jnp.zeros((orb, LANES), F32)
        accs = lax.fori_loop(0, ny // un, body, (zero,) * slots)
        for s in range(slots):
            sums[p * slots + s] = accs[s]
    parts = [[sums[p * slots + s] for s in range(slots)] for p in range(SLAB)]
    tile = coef_tile(parts, slots, atom_dev)
    tile_out[...] = tile
    put_edges(ny, atom_dev, field, tile, inner, outer)


def step_kernel(kind, ny, atom_dev, *refs):
    slots = 3 * atom_dev
    refs = list(refs)
    zsum = refs.pop()
    take = lambda count: [refs.pop(0) for _ in range(count)]
    consts, dense, field, tile_in, inside, outside = take(6)
    if kind == "b1":
        (other,) = take(1)
    elif kind == "t2":
        other, full_zero, b1, tile_b1, b2, tile_b2, cot, full_cot = take(8)
    elif kind == "out":
        other, cot, gp, e, e_inside, e_outside = take(6)
    if kind in ("b2", "t1"):
        new, tile_out, inner, outer, full_out = refs
    elif kind == "b1":
        new, tile_out, inner, outer = refs
    elif kind == "t2":
        gp, e_out, e_inner, e_outer = refs
    else:
        (new,) = refs
    orb = field.shape[1]
    full = tile_in[...] + inside[ny] + outside[ny]
    if kind in ("b2", "t1"):
        full_out[...] = full
    near = NEAR * atom_dev
    c0, c1, c2, c3 = [consts[near + n : near + n + 1, :] for n in range(4)]
    keep, scale, mix = {
        "t1": (None, 1.0, None),
        "t2": (None, 2.0, -1.0),
        "b2": (c2, 2.0 * c3, None),
        "b1": (None, 2.0, c1 - c3),
        "out": (None, 1.0, -1.0),
    }[kind]
    spread = []
    for t in range(near):
        coupling = consts[t : t + 1, :] * scale
        spread.append(jnp.broadcast_to(full[:, t : t + 1], (orb, LANES)) * coupling)
    side = scale * (-0.5 / spectral_half)
    sums = []
    part = (orb + 1) * ny + 8
    lane, line = (lax.broadcasted_iota(jnp.int32, (2 * LANES, LANES), d) for d in (1, 0))
    apart = (lane - line) % LANES
    turn = jnp.where((apart == 1) | (apart == LANES - 1), 1.0, 0.0).astype(jnp.bfloat16)
    for p in range(SLAB):
        flat = field[p * ny : (p + 1) * ny].reshape(orb * ny, LANES)
        high = flat.astype(jnp.bfloat16)
        low = (flat - high.astype(F32)).astype(jnp.bfloat16)
        zsum[p * ny : (p + 1) * ny] = jnp.dot(
            jnp.concatenate([high, low], axis=1), turn, preferred_element_type=F32
        ).reshape(ny, orb, LANES)
    un = ny
    for p in range(SLAB):

        def body(yb, accs, p=p):
            accs = list(accs)
            rows = []
            first = yb * un
            before = p * ny + jnp.where(first == 0, ny - 1, first - 1)
            after = p * ny + jnp.where(first == ny - un, 0, first + un)
            lines = [field[before]] + [field[p * ny + first + yy] for yy in range(un)]
            lines.append(field[after])
            for yy in range(un):
                y = first + yy
                row = p * ny + y
                earlier, v, later = lines[yy : yy + 3]
                beyond = (outside if p else inside)[y] + field[(1 - p) * ny + y]
                beside = (later + earlier) + (beyond + zsum[row])
                pot = dense[row, slots : slots + 1, :] * scale
                if keep is not None:
                    pot = pot + keep
                weights = [dense[row, s : s + 1, :] for s in range(slots)]
                a = [spread[p * atom_dev + s] * weights[s] for s in range(slots)]
                while len(a) > 1:
                    a = [sum(a[n + 1 : n + 2], a[n]) for n in range(0, len(a), 2)]
                x = v * pot + beside * side + a[0]
                if mix is not None:
                    x = x + other[row] * mix
                if kind == "out":
                    x = x + cot[row] * c0
                    new[pl.ds(p * part + y, orb, stride=ny), :] = x
                elif kind == "t2":
                    g = b1[row] * other[row] + 2.0 * (b2[row] * v)
                    g = g + (2.0 * c3) * (cot[row] * x)
                    rows.append(jnp.sum(g, axis=0, keepdims=True))
                else:
                    new[row] = x
                if kind != "out":
                    for s in range(slots):
                        accs[s] = accs[s] + x * weights[s]
            if kind == "t2":
                start = pl.multiple_of(p * ny + yb * un, un)
                gp[pl.ds(start, un), :] = jnp.concatenate(rows, axis=0) * (1.0 / spectral_half)
            return tuple(accs)

        zero = jnp.zeros((orb, LANES), F32)
        init = () if kind == "out" else (zero,) * slots
        sums.append(lax.fori_loop(0, ny // un, body, init))
    if kind == "out":
        total = e[...] + e_inside[...] + e_outside[...]
        for p in range(SLAB):
            rest = p * part + orb * ny
            new[rest : rest + ny, :] = gp[p * ny : (p + 1) * ny, :]
            new[rest + ny : rest + ny + 8, :] = pltpu.roll(total, LANES - (p + 1) * atom_dev, 1)
        return
    tile = coef_tile(sums, slots, atom_dev)
    if kind == "t2":
        e = tile_b1[...] * full_zero[...] + 2.0 * (tile_b2[...] * full)
        e = e + (2.0 * c3) * (full_cot[...] * tile)
        e = jnp.sum(e, axis=0, keepdims=True) * (1.0 / spectral_half)
        e = jnp.broadcast_to(e, (8, LANES))
        e_out[...] = e
        lane = lane_iota(e.shape)
        mine = (lane >= atom_dev) & (lane < 2 * atom_dev)
        e_inner[...] = jnp.where(mine, pltpu.roll(e, atom_dev, 1), 0.0)
        mine = (lane >= 2 * atom_dev) & (lane < 3 * atom_dev)
        e_outer[...] = jnp.where(mine, pltpu.roll(e, LANES - atom_dev, 1), 0.0)
        return
    tile_out[...] = tile
    put_edges(ny, atom_dev, new, tile, inner, outer)


def final_kernel(ny, orb, atom_dev, idx, *refs):
    blocks, (out, gp_out, e_out, gp, e_box, sems) = refs[:2], refs[2:]
    k = lax.rem(idx[0], GROUP)
    rows = orb * ny
    copies = []
    for n in range(2):
        first = pl.multiple_of((lax.rem(k, 2) ^ (1 - n)) * rows, rows)
        copies.append(
            pltpu.make_async_copy(
                blocks[n].at[pl.ds(0, rows)], out.at[pl.ds(first, rows)], sems.at[n]
            )
        )
    for copy in copies:
        copy.start()
    total = blocks[0][rows:, :] + blocks[1][rows:, :]
    gp[...] = total[0:ny]
    last = pltpu.make_async_copy(gp, gp_out, sems.at[2])
    last.start()
    e = total[ny : ny + 1]
    lane = lane_iota(e.shape)
    for n in range(atom_dev):
        e_box[n] = jnp.sum(jnp.where(lane == n, e, 0.0))
    ends = [last, pltpu.make_async_copy(e_box, e_out, sems.at[3])]
    ends[1].start()
    for copy in copies + ends:
        copy.wait()


def per_device(orbitals, cotangent, potential, cheb_coef, energy, proj_cell, proj_atom, proj_value):
    orb_all, _, ny, nz = orbitals.shape
    devices = lax.axis_size("grid")
    groups = devices // GROUP
    atoms = energy.shape[0]
    atom_dev = atoms // devices
    points = proj_cell.shape[0] // LANES
    orb = orb_all // 2
    assert orb % 8 == 0 and nz == LANES and devices % GROUP == 0
    idx = lax.axis_index("grid").astype(jnp.int32).reshape(1)
    block = orb * ny
    plane = SLAB * ny

    def pairs(within):
        return [(GROUP * g + a, GROUP * g + b) for g in range(groups) for a, b in within]

    enter = [(0, 2), (1, 0), (2, 3), (3, 1)]
    leave = [(b, a) for a, b in enter]
    swap = [(0, 0), (1, 2), (2, 1), (3, 3)]
    core = pairs([(0, 1), (1, 0), (2, 3), (3, 2)])
    across = []
    for g in range(groups):
        for m in range(2):
            below, above = GROUP * g + 2 * m + 1, GROUP * ((g + 1) % groups) + 2 * m
            across += [(below, above), (above, below)]

    def permute(x, to):
        return lax.ppermute(x, "grid", to)

    def halo(inner, outer):
        beyond = permute(outer, across)
        return permute(inner, core), beyond

    def exchange(blocks, first):
        return [permute(blocks[0], pairs(first)), permute(blocks[1], pairs(swap))]

    consts, *blocks = call(
        functools.partial(prep_kernel, devices, atoms),
        [(-(-(NEAR * atom_dev + 4) // 8) * 8, LANES)] + [(block + 3 * points + ny, LANES)] * 2,
        idx,
        cheb_coef,
        energy,
        proj_cell.reshape(points, LANES),
        proj_atom.reshape(points, LANES),
        proj_value.reshape(points, LANES),
        potential.reshape(ny, LANES),
        cotangent.reshape(orb_all * ny, LANES),
        micros=1.2,
        scratch=[
            pltpu.VMEM((2, points, LANES), jnp.int32),
            pltpu.SMEM(cheb_coef.shape, F32),
            pltpu.SMEM(energy.shape, F32),
            pltpu.VMEM((points, LANES), F32),
            pltpu.VMEM((ny, LANES), F32),
            pltpu.SemaphoreType.DMA((8,)),
        ],
        smem=(0,),
        hbm_args=range(1, 8),
    )
    cot_blocks = exchange(blocks, enter)
    blocks = call(
        pack_kernel,
        [(block, LANES)] * 2,
        idx,
        orbitals.reshape(orb_all * ny, LANES),
        micros=1.0,
        scratch=[pltpu.SemaphoreType.DMA((2,))],
        smem=(0,),
        hbm_args=(1,),
    )
    orb_blocks = exchange(blocks, enter)
    field_shape, tile_shape = (plane, orb, LANES), (orb, LANES)
    edge_shape, sums_shape = (ny + 1, orb, LANES), (8, LANES)
    chain = [field_shape, tile_shape, edge_shape, edge_shape]

    def relay(first, blocks, *args):
        return call(
            functools.partial(relay_kernel, ny, orb, atom_dev, first),
            ([(plane, 8, LANES)] if first else []) + chain,
            idx,
            *blocks,
            *args,
            micros=1.4 if first else 0.7,
            scratch=[pltpu.VMEM((SLAB * 3 * atom_dev, orb, LANES), F32)],
            smem=(0,),
        )

    def step(kind, outs, *args):
        return call(
            functools.partial(step_kernel, kind, ny, atom_dev),
            outs,
            consts,
            dense,
            *args,
            micros=1.0,
            scratch=[pltpu.VMEM(field_shape, F32)],
        )

    dense, cot, tile_cot, *edges = relay(True, cot_blocks)
    inner, outer = edges
    cot_halo = halo(inner, outer)
    cot_halo = (
        jnp.concatenate([permute(inner[:ny], core), permute(inner[ny:], core)]),
        cot_halo[1],
    )
    zero, tile_zero, *edges = relay(False, orb_blocks, dense)
    zero_halo = halo(*edges)
    b2, tile_b2, *edges, full_cot = step("b2", chain + [tile_shape], cot, tile_cot, *cot_halo)
    b2_halo = halo(*edges)
    t1, tile_t1, *edges, full_zero = step("t1", chain + [tile_shape], zero, tile_zero, *zero_halo)
    t1_halo = halo(*edges)
    b1, tile_b1, *edges = step("b1", chain, b2, tile_b2, *b2_halo, cot)
    b1_halo = halo(*edges)
    gp, e, *edges = step(
        "t2",
        [(plane, LANES)] + [sums_shape] * 3,
        t1,
        tile_t1,
        *t1_halo,
        zero,
        full_zero,
        b1,
        tile_b1,
        b2,
        tile_b2,
        cot,
        full_cot,
    )
    part = block + ny + 8
    (image,) = step(
        "out", [(SLAB * part, LANES)], b1, tile_b1, *b1_halo, b2, cot, gp, e, *halo(*edges)
    )
    place = first_place(lax.rem(idx[0], GROUP))
    images = exchange(
        [
            lax.dynamic_slice_in_dim(image, place * part, part, 0),
            lax.dynamic_slice_in_dim(image, (1 - place) * part, part, 0),
        ],
        leave,
    )
    out, gp, e = call(
        functools.partial(final_kernel, ny, orb, atom_dev),
        [(orb_all * ny, LANES), (ny, LANES), (atom_dev,)],
        idx,
        *images,
        micros=1.0,
        scratch=[
            pltpu.VMEM((ny, LANES), F32),
            pltpu.SMEM((atom_dev,), F32),
            pltpu.SemaphoreType.DMA((4,)),
        ],
        smem=(0,),
        hbm_outs=(0, 1, 2),
    )
    return out.reshape(orbitals.shape), gp.reshape(potential.shape), e


def solution(mesh):
    placed = (
        P("sample", "grid", None, None),
        P("sample", "grid", None, None),
        P("grid", None, None),
        P(),
        P(),
        P("grid"),
        P("grid"),
        P("grid"),
    )
    return jax.shard_map(
        per_device,
        mesh=mesh,
        in_specs=placed,
        out_specs=(
            P("sample", "grid", None, None),
            P(("sample", "grid"), None, None),
            P(("sample", "grid")),
        ),
        check_vma=False,
    )
```

```python
import functools

import jax
import jax.numpy as jnp
from jax import lax
from jax.experimental import pallas as pl
from jax.experimental.pallas import tpu as pltpu
from jax.sharding import PartitionSpec as P

spectral_center = 4.5
spectral_half = 4.5

GROUP = 4
SLAB = 2
NEAR = SLAB + 2
LANES = 128
F32 = jnp.float32


def call(body, outs, *args, micros, scratch=(), smem=(), hbm_args=(), hbm_outs=(), smem_outs=()):
    in_specs, operands = [], []
    for n, a in enumerate(args):
        if n in smem:
            in_specs.append(pl.BlockSpec(memory_space=pltpu.SMEM))
        elif n in hbm_args:
            in_specs.append(pl.BlockSpec(memory_space=pltpu.HBM))
            a = pltpu.with_memory_space_constraint(a, pltpu.HBM)
        else:
            in_specs.append(pl.BlockSpec(memory_space=pltpu.VMEM))
            a = pltpu.with_memory_space_constraint(a, pltpu.VMEM)
        operands.append(a)
    out_shape, out_specs = [], []
    for n, shape in enumerate(outs):
        if n in hbm_outs:
            out_shape.append(jax.ShapeDtypeStruct(shape, F32))
            out_specs.append(pl.BlockSpec(memory_space=pltpu.HBM))
        elif n in smem_outs:
            out_shape.append(jax.ShapeDtypeStruct(shape, F32))
            out_specs.append(pl.BlockSpec(memory_space=pltpu.SMEM))
        else:
            out_shape.append(pltpu.VMEM(shape, F32))
            out_specs.append(pl.BlockSpec(memory_space=pltpu.VMEM))
    return pl.pallas_call(
        body,
        out_shape=out_shape,
        in_specs=in_specs,
        out_specs=out_specs,
        scratch_shapes=list(scratch),
        compiler_params=pltpu.CompilerParams(vmem_limit_bytes=16 << 20),
        cost_estimate=pl.CostEstimate(
            flops=int(micros * 1e6), bytes_accessed=int(micros * 3.69e6), transcendentals=0
        ),
    )(*operands)


def lane_iota(shape):
    return lax.broadcasted_iota(jnp.int32, shape, len(shape) - 1)


def prep_kernel(devices, atoms, idx, cheb, energy, cell, atom, value, pot, cot, *refs):
    consts, blocks = refs[0], refs[1:3]
    box, cheb_box, energy_box, value_box, pot_box, sems = refs[3:]
    count, ny = cell.shape[0], pot.shape[0]
    rows = blocks[0].shape[0] - 3 * count - ny
    atom_dev = atoms // devices
    k = lax.rem(idx[0], GROUP)
    moves = [(cell, box.at[0]), (atom, box.at[1]), (cheb, cheb_box), (energy, energy_box)]
    moves += [(value, value_box), (pot, pot_box)]
    for n in range(2):
        first = pl.multiple_of((lax.rem(k, 2) ^ (1 - n)) * rows, rows)
        moves.append((cot.at[pl.ds(first, rows)], blocks[n].at[pl.ds(0, rows)]))
    copies = [
        pltpu.make_async_copy(src, dst, sems.at[n]) for n, (src, dst) in enumerate(moves)
    ]
    for copy in copies[::-1]:
        copy.start()
    for copy in copies[:6]:
        copy.wait()
    up = lax.rem(k, 2) == 1
    first_plane = idx[0] - k + lax.rem(k, 2) * SLAB - 1
    for t in range(NEAR * atom_dev):
        h, r = t // atom_dev, t % atom_dev
        a = (first_plane + jnp.where(up, h, NEAR - 1 - h)) * atom_dev + r
        a = jnp.where(a < 0, a + atoms, jnp.where(a >= atoms, a - atoms, a))
        consts[t : t + 1, :] = jnp.full((1, LANES), energy_box[a] * (1.0 / spectral_half), F32)
    for n in range(4):
        at = NEAR * atom_dev + n
        consts[at : at + 1, :] = jnp.full((1, LANES), cheb_box[n], F32)
    shifted = box[1] + (atoms - (idx[0] - 1) * atom_dev)
    shifted = jnp.where(shifted >= 2 * atoms, shifted - 2 * atoms, shifted)
    slot = jnp.where(shifted >= atoms, shifted - atoms, shifted)
    home = jnp.where(slot >= 2 * atom_dev, 2, jnp.where(slot >= atom_dev, 1, 0))
    slot = jnp.where(k >= 2, slot, slot + (2 - 2 * home) * atom_dev)
    for block in blocks:
        at = rows
        for part in (value_box[...], pot_box[...], box[0].astype(F32), slot.astype(F32)):
            block[at : at + part.shape[0], :] = part
            at += part.shape[0]
    for copy in copies[6:]:
        copy.wait()


def pack_kernel(idx, field, *refs):
    blocks, sems = refs[:2], refs[2]
    rows = blocks[0].shape[0]
    k = lax.rem(idx[0], GROUP)
    copies = []
    for n in range(2):
        first = pl.multiple_of((lax.rem(k, 2) ^ (1 - n)) * rows, rows)
        copies.append(
            pltpu.make_async_copy(field.at[pl.ds(first, rows)], blocks[n], sems.at[n])
        )
    for copy in copies:
        copy.start()
        copy.wait()


def first_place(k):
    return jnp.where((k == 1) | (k == 2), 1, 0)


def fill_dense(ny, slots, block, places, ins, out):
    rows = (ins[0].shape[0] - block - ny) // 3
    rest = block + rows + ny
    half = jnp.bfloat16
    place = lax.broadcasted_iota(jnp.int32, (ny * 8, LANES), 0).astype(F32).astype(half)
    column = lax.broadcasted_iota(jnp.int32, (LANES, LANES), 0).astype(F32).astype(half)
    one, none = jnp.ones((), half), jnp.zeros((), half)
    for p, src in zip(places, ins):
        cell = src[rest : rest + rows, :]
        line = jnp.floor(cell * (1.0 / LANES))
        z = (cell - line * LANES).astype(half)
        code = (line * 8 + src[rest + rows : rest + 2 * rows, :]).astype(half)
        value = src[block : block + rows, :]
        high = value.astype(half)
        low = (value - high.astype(F32)).astype(half)
        left, right = [], []
        for r in range(rows):
            left.append(jnp.where(place == code[r : r + 1, :], one, none))
            hit = column == z[r : r + 1, :]
            right.append(
                jnp.concatenate(
                    [jnp.where(hit, piece[r : r + 1, :], none) for piece in (high, low)], axis=0
                )
            )
        both = lax.dot_general(
            jnp.concatenate(left, axis=1),
            jnp.concatenate(right, axis=1),
            (((1,), (1,)), ((), ())),
            preferred_element_type=F32,
        )
        dense = both[:, :LANES] + both[:, LANES:]
        first = pl.multiple_of(p * ny, ny)
        out[pl.ds(first, ny)] = dense.reshape(ny, 8, LANES)
        pot = (src[block + rows : rest, :] - (spectral_center - 3.0)) * (1.0 / spectral_half)
        out[pl.ds(first, ny), slots : slots + 1, :] = pot.reshape(ny, 1, LANES)


def edge_tiles(tile, atom_dev):
    lane = lane_iota(tile.shape)
    earlier, later = pltpu.roll(tile, atom_dev, 1), pltpu.roll(tile, LANES - atom_dev, 1)
    turned = jnp.where(lax.rem(lane, 2 * atom_dev) < atom_dev, later, earlier)
    inner = jnp.where(lane < 2 * atom_dev, turned, 0.0)
    outer = jnp.where((lane >= 2 * atom_dev) & (lane < 4 * atom_dev), turned, 0.0)
    return inner, outer


def coef_tile(sums, slots, atom_dev):
    shape = sums[0][0].shape
    lane = lane_iota(shape)
    tile = jnp.zeros(shape, F32)
    for t in range(NEAR * atom_dev):
        total = None
        for p in range(SLAB):
            slot = t - p * atom_dev
            if 0 <= slot < slots:
                total = sums[p][slot] if total is None else total + sums[p][slot]
        tile = jnp.where(lane == t, jnp.sum(total, axis=1, keepdims=True), tile)
    return tile


def put_edges(ny, atom_dev, field, tile, inner, outer):
    inner[ny], outer[ny] = edge_tiles(tile, atom_dev)
    inner[0:ny] = field[0:ny]
    outer[0:ny] = field[ny : 2 * ny]


def relay_kernel(ny, orb, atom_dev, first, idx, *refs):
    slots = 3 * atom_dev
    ins, (dense, field, tile_out, inner, outer, sums) = refs[:2], refs[2:]
    place = first_place(lax.rem(idx[0], GROUP))
    places = (place, 1 - place)
    if first:
        fill_dense(ny, slots, orb * ny, places, ins, dense)
    un = 8
    for p, src in zip(places, ins):

        def body(yb, accs, src=src, p=p):
            accs = list(accs)
            for yy in range(un):
                y = yb * un + yy
                v = src[pl.ds(y, orb, stride=ny), :]
                row = p * ny + y
                field[row] = v
                for s in range(slots):
                    accs[s] = accs[s] + v * dense[row, s : s + 1, :]
            return tuple(accs)

        zero = jnp.zeros((orb, LANES), F32)
        accs = lax.fori_loop(0, ny // un, body, (zero,) * slots)
        for s in range(slots):
            sums[p * slots + s] = accs[s]
    parts = [[sums[p * slots + s] for s in range(slots)] for p in range(SLAB)]
    tile = coef_tile(parts, slots, atom_dev)
    tile_out[...] = tile
    put_edges(ny, atom_dev, field, tile, inner, outer)


def step_kernel(kind, ny, atom_dev, *refs):
    slots = 3 * atom_dev
    refs = list(refs)
    zsum = refs.pop()
    take = lambda count: [refs.pop(0) for _ in range(count)]
    consts, dense, field, tile_in, inside, outside = take(6)
    if kind == "b1":
        (other,) = take(1)
    elif kind == "t2":
        other, full_zero, b1, tile_b1, b2, tile_b2, cot, full_cot = take(8)
    elif kind == "out":
        other, cot, gp, e, e_inside, e_outside = take(6)
    if kind in ("b2", "t1"):
        new, tile_out, inner, outer, full_out = refs
    elif kind == "b1":
        new, tile_out, inner, outer = refs
    elif kind == "t2":
        gp, e_out, e_inner, e_outer = refs
    else:
        (new,) = refs
    orb = field.shape[1]
    full = tile_in[...] + inside[ny] + outside[ny]
    if kind in ("b2", "t1"):
        full_out[...] = full
    near = NEAR * atom_dev
    c0, c1, c2, c3 = [consts[near + n : near + n + 1, :] for n in range(4)]
    keep, scale, mix = {
        "t1": (None, 1.0, None),
        "t2": (None, 2.0, -1.0),
        "b2": (c2, 2.0 * c3, None),
        "b1": (None, 2.0, c1 - c3),
        "out": (None, 1.0, -1.0),
    }[kind]
    spread = []
    for t in range(near):
        coupling = consts[t : t + 1, :] * scale
        spread.append(jnp.broadcast_to(full[:, t : t + 1], (orb, LANES)) * coupling)
    side = scale * (-0.5 / spectral_half)
    sums = []
    part = (orb + 1) * ny + 8
    lane, line = (lax.broadcasted_iota(jnp.int32, (2 * LANES, LANES), d) for d in (1, 0))
    apart = (lane - line) % LANES
    turn = jnp.where((apart == 1) | (apart == LANES - 1), 1.0, 0.0).astype(jnp.bfloat16)
    for p in range(SLAB):
        flat = field[p * ny : (p + 1) * ny].reshape(orb * ny, LANES)
        high = flat.astype(jnp.bfloat16)
        low = (flat - high.astype(F32)).astype(jnp.bfloat16)
        zsum[p * ny : (p + 1) * ny] = jnp.dot(
            jnp.concatenate([high, low], axis=1), turn, preferred_element_type=F32
        ).reshape(ny, orb, LANES)
    un = ny
    for p in range(SLAB):

        def body(yb, accs, p=p):
            accs = list(accs)
            rows = []
            first = yb * un
            before = p * ny + jnp.where(first == 0, ny - 1, first - 1)
            after = p * ny + jnp.where(first == ny - un, 0, first + un)
            lines = [field[before]] + [field[p * ny + first + yy] for yy in range(un)]
            lines.append(field[after])
            for yy in range(un):
                y = first + yy
                row = p * ny + y
                earlier, v, later = lines[yy : yy + 3]
                beyond = (outside if p else inside)[y] + field[(1 - p) * ny + y]
                beside = (later + earlier) + (beyond + zsum[row])
                pot = dense[row, slots : slots + 1, :] * scale
                if keep is not None:
                    pot = pot + keep
                weights = [dense[row, s : s + 1, :] for s in range(slots)]
                a = [spread[p * atom_dev + s] * weights[s] for s in range(slots)]
                while len(a) > 1:
                    a = [sum(a[n + 1 : n + 2], a[n]) for n in range(0, len(a), 2)]
                x = v * pot + beside * side + a[0]
                if mix is not None:
                    x = x + other[row] * mix
                if kind == "out":
                    x = x + cot[row] * c0
                    new[pl.ds(p * part + y, orb, stride=ny), :] = x
                elif kind == "t2":
                    g = b1[row] * other[row] + 2.0 * (b2[row] * v)
                    g = g + (2.0 * c3) * (cot[row] * x)
                    rows.append(jnp.sum(g, axis=0, keepdims=True))
                else:
                    new[row] = x
                if kind != "out":
                    for s in range(slots):
                        accs[s] = accs[s] + x * weights[s]
            if kind == "t2":
                start = pl.multiple_of(p * ny + yb * un, un)
                gp[pl.ds(start, un), :] = jnp.concatenate(rows, axis=0) * (1.0 / spectral_half)
            return tuple(accs)

        zero = jnp.zeros((orb, LANES), F32)
        init = () if kind == "out" else (zero,) * slots
        sums.append(lax.fori_loop(0, ny // un, body, init))
    if kind == "out":
        total = e[...] + e_inside[...] + e_outside[...]
        for p in range(SLAB):
            rest = p * part + orb * ny
            new[rest : rest + ny, :] = gp[p * ny : (p + 1) * ny, :]
            new[rest + ny : rest + ny + 8, :] = pltpu.roll(total, LANES - (p + 1) * atom_dev, 1)
        return
    tile = coef_tile(sums, slots, atom_dev)
    if kind == "t2":
        e = tile_b1[...] * full_zero[...] + 2.0 * (tile_b2[...] * full)
        e = e + (2.0 * c3) * (full_cot[...] * tile)
        e = jnp.sum(e, axis=0, keepdims=True) * (1.0 / spectral_half)
        e = jnp.broadcast_to(e, (8, LANES))
        e_out[...] = e
        lane = lane_iota(e.shape)
        mine = (lane >= atom_dev) & (lane < 2 * atom_dev)
        e_inner[...] = jnp.where(mine, pltpu.roll(e, atom_dev, 1), 0.0)
        mine = (lane >= 2 * atom_dev) & (lane < 3 * atom_dev)
        e_outer[...] = jnp.where(mine, pltpu.roll(e, LANES - atom_dev, 1), 0.0)
        return
    tile_out[...] = tile
    put_edges(ny, atom_dev, new, tile, inner, outer)


def final_kernel(ny, orb, atom_dev, idx, *refs):
    blocks, (out, gp_out, e_out, gp, e_box, sems) = refs[:2], refs[2:]
    k = lax.rem(idx[0], GROUP)
    rows = orb * ny
    copies = []
    for n in range(2):
        first = pl.multiple_of((lax.rem(k, 2) ^ (1 - n)) * rows, rows)
        copies.append(
            pltpu.make_async_copy(
                blocks[n].at[pl.ds(0, rows)], out.at[pl.ds(first, rows)], sems.at[n]
            )
        )
    for copy in copies:
        copy.start()
    total = blocks[0][rows:, :] + blocks[1][rows:, :]
    gp[...] = total[0:ny]
    last = pltpu.make_async_copy(gp, gp_out, sems.at[2])
    last.start()
    e = total[ny : ny + 1]
    lane = lane_iota(e.shape)
    for n in range(atom_dev):
        e_box[n] = jnp.sum(jnp.where(lane == n, e, 0.0))
    ends = [last, pltpu.make_async_copy(e_box, e_out, sems.at[3])]
    ends[1].start()
    for copy in copies + ends:
        copy.wait()


def per_device(orbitals, cotangent, potential, cheb_coef, energy, proj_cell, proj_atom, proj_value):
    orb_all, _, ny, nz = orbitals.shape
    devices = lax.axis_size("grid")
    groups = devices // GROUP
    atoms = energy.shape[0]
    atom_dev = atoms // devices
    points = proj_cell.shape[0] // LANES
    orb = orb_all // 2
    assert orb % 8 == 0 and nz == LANES and devices % GROUP == 0
    idx = lax.axis_index("grid").astype(jnp.int32).reshape(1)
    block = orb * ny
    plane = SLAB * ny

    def pairs(within):
        return [(GROUP * g + a, GROUP * g + b) for g in range(groups) for a, b in within]

    enter = [(0, 2), (1, 0), (2, 3), (3, 1)]
    leave = [(b, a) for a, b in enter]
    swap = [(0, 0), (1, 2), (2, 1), (3, 3)]
    core = pairs([(0, 1), (1, 0), (2, 3), (3, 2)])
    across = []
    for g in range(groups):
        for m in range(2):
            below, above = GROUP * g + 2 * m + 1, GROUP * ((g + 1) % groups) + 2 * m
            across += [(below, above), (above, below)]

    def permute(x, to):
        return lax.ppermute(x, "grid", to)

    def halo(inner, outer):
        beyond = permute(outer, across)
        return permute(inner, core), beyond

    def exchange(blocks, first):
        return [permute(blocks[0], pairs(first)), permute(blocks[1], pairs(swap))]

    consts, *blocks = call(
        functools.partial(prep_kernel, devices, atoms),
        [(-(-(NEAR * atom_dev + 4) // 8) * 8, LANES)] + [(block + 3 * points + ny, LANES)] * 2,
        idx,
        cheb_coef,
        energy,
        proj_cell.reshape(points, LANES),
        proj_atom.reshape(points, LANES),
        proj_value.reshape(points, LANES),
        potential.reshape(ny, LANES),
        cotangent.reshape(orb_all * ny, LANES),
        micros=1.2,
        scratch=[
            pltpu.VMEM((2, points, LANES), jnp.int32),
            pltpu.SMEM(cheb_coef.shape, F32),
            pltpu.SMEM(energy.shape, F32),
            pltpu.VMEM((points, LANES), F32),
            pltpu.VMEM((ny, LANES), F32),
            pltpu.SemaphoreType.DMA((8,)),
        ],
        smem=(0,),
        hbm_args=range(1, 8),
    )
    cot_blocks = exchange(blocks, enter)
    blocks = call(
        pack_kernel,
        [(block, LANES)] * 2,
        idx,
        orbitals.reshape(orb_all * ny, LANES),
        micros=1.0,
        scratch=[pltpu.SemaphoreType.DMA((2,))],
        smem=(0,),
        hbm_args=(1,),
    )
    orb_blocks = exchange(blocks, enter)
    field_shape, tile_shape = (plane, orb, LANES), (orb, LANES)
    edge_shape, sums_shape = (ny + 1, orb, LANES), (8, LANES)
    chain = [field_shape, tile_shape, edge_shape, edge_shape]

    def relay(first, blocks, *args):
        return call(
            functools.partial(relay_kernel, ny, orb, atom_dev, first),
            ([(plane, 8, LANES)] if first else []) + chain,
            idx,
            *blocks,
            *args,
            micros=1.4 if first else 0.7,
            scratch=[pltpu.VMEM((SLAB * 3 * atom_dev, orb, LANES), F32)],
            smem=(0,),
        )

    def step(kind, outs, *args):
        return call(
            functools.partial(step_kernel, kind, ny, atom_dev),
            outs,
            consts,
            dense,
            *args,
            micros=1.0,
            scratch=[pltpu.VMEM(field_shape, F32)],
        )

    dense, cot, tile_cot, *edges = relay(True, cot_blocks)
    inner, outer = edges
    cot_halo = halo(inner, outer)
    cot_halo = (
        jnp.concatenate([permute(inner[:ny], core), permute(inner[ny:], core)]),
        cot_halo[1],
    )
    zero, tile_zero, *edges = relay(False, orb_blocks, dense)
    zero_halo = halo(*edges)
    b2, tile_b2, *edges, full_cot = step("b2", chain + [tile_shape], cot, tile_cot, *cot_halo)
    b2_halo = halo(*edges)
    t1, tile_t1, *edges, full_zero = step("t1", chain + [tile_shape], zero, tile_zero, *zero_halo)
    t1_halo = halo(*edges)
    b1, tile_b1, *edges = step("b1", chain, b2, tile_b2, *b2_halo, cot)
    b1_halo = halo(*edges)
    gp, e, *edges = step(
        "t2",
        [(plane, LANES)] + [sums_shape] * 3,
        t1,
        tile_t1,
        *t1_halo,
        zero,
        full_zero,
        b1,
        tile_b1,
        b2,
        tile_b2,
        cot,
        full_cot,
    )
    part = block + ny + 8
    (image,) = step(
        "out", [(SLAB * part, LANES)], b1, tile_b1, *b1_halo, b2, cot, gp, e, *halo(*edges)
    )
    place = first_place(lax.rem(idx[0], GROUP))
    images = exchange(
        [
            lax.dynamic_slice_in_dim(image, place * part, part, 0),
            lax.dynamic_slice_in_dim(image, (1 - place) * part, part, 0),
        ],
        leave,
    )
    out, gp, e = call(
        functools.partial(final_kernel, ny, orb, atom_dev),
        [(orb_all * ny, LANES), (ny, LANES), (atom_dev,)],
        idx,
        *images,
        micros=1.0,
        scratch=[
            pltpu.VMEM((ny, LANES), F32),
            pltpu.SMEM((atom_dev,), F32),
            pltpu.SemaphoreType.DMA((4,)),
        ],
        smem=(0,),
        hbm_outs=(0, 1, 2),
    )
    return out.reshape(orbitals.shape), gp.reshape(potential.shape), e


def solution(mesh):
    placed = (
        P("sample", "grid", None, None),
        P("sample", "grid", None, None),
        P("grid", None, None),
        P(),
        P(),
        P("grid"),
        P("grid"),
        P("grid"),
    )
    return jax.shard_map(
        per_device,
        mesh=mesh,
        in_specs=placed,
        out_specs=(
            P("sample", "grid", None, None),
            P(("sample", "grid"), None, None),
            P(("sample", "grid")),
        ),
        check_vma=False,
    )
```
